512 devices in a mesh: island: 8 (over y_hi, x), local: 64 (over z, y_lo, core).
Axes of the slice: x: 4, y: 4 (y_hi: 2, y_lo: 2; y = y_hi * 2 + y_lo), z: 16, core: 2. Of those that a mesh axis runs over, the one named last changes fastest.
Arguments:
- activations: bfloat16 [65536, 4096], P(('island', 'local')), may hold values from -8 to 8
- norm_gain: float32 [4096], replicated, may hold values from 0.25 to 1.75
- qkv_weight: bfloat16 [4096, 384], P('local'), may hold values from -3 to 3
- positions: int32 [65536], P(('island', 'local')), may hold values from 0 to 127, as said below
- cotangent: bfloat16 [65536, 128], P(('island', 'local')), may hold values from -0.0625 to 0.0625
Outputs:
- qkv_gradient: float32 [4096, 384], P(('island', 'local'))
- gain_gradient: float32 [4096], P(('island', 'local'))
The draws below stay inside these ranges and needn't reach their ends.
Inputs may be any that keep to these rules, and one draw needn't show every extreme that they name: `positions`: every block of 128 tokens begins a document with position 0; within a block a position is one more than the one before it or 0 where a new document starts; in some block no new document starts.
All inputs are finite; a program needn't handle non-finite values.
Results may differ from the reference program's by a relative error of at most 0.007.
The reference program's roundings to bfloat16 on the way (of `normed`, `attention_low`, `score_grad` and `qkv_grads`) count: a program that leaves them out, or rounds other values in their place, can miss the bound.
Values may be sent and summed in bfloat16 or wider, within the bound.
No kernel may reach another device: no remote copies, remote signals or barrier semaphores. Data moves between devices by JAX's collectives and lax.ppermute only.
A program may use at most 64 MiB of HBM per device.

```python
import jax
import jax.numpy as jnp
from jax import lax

D = 4096
HD = 128
TOK_DEV = 128
TOKENS = 65536


def draw_activations(key, part):
    key = jax.random.fold_in(key, 11)
    first_key = jax.random.fold_in(key, 0)
    drawn = jnp.clip(jax.random.normal(first_key, (TOKENS, D), jnp.float32), -6.0, 6.0)
    return drawn.astype(jnp.bfloat16)


def draw_qkv_weight(key, part):
    key = jax.random.fold_in(key, 13)
    first_key = jax.random.fold_in(key, 0)
    drawn = jnp.clip(jax.random.normal(first_key, (D, 3 * HD), jnp.float32), -6.0, 6.0) * D ** (-0.5)
    return drawn.astype(jnp.bfloat16)


def draw_positions(key, part):
    key = jax.random.fold_in(key, 17)
    first_key, second_key = jax.random.split(key)
    token_index = jnp.arange(TOKENS, dtype=jnp.int32)
    starts = jax.random.randint(first_key, (TOKENS,), 0, 96) == 0
    whole_block = jax.random.randint(second_key, (), 0, TOKENS // TOK_DEV)
    in_whole = token_index // TOK_DEV == whole_block
    starts = starts & jnp.logical_not(in_whole) | (token_index % TOK_DEV == 0)
    marked = jnp.where(starts, token_index, 0)
    return token_index - lax.cummax(marked, axis=0)


def shard_levels(rng, shape, pieces, low, high):
    level = 1.0
    for position, shards_of in pieces:
        steps = jax.random.uniform(jax.random.fold_in(jax.random.fold_in(rng, 6), position), (shards_of,), jnp.float32, low / len(pieces), high / len(pieces))
        level = level * jnp.repeat(jnp.exp(steps), shape[position] // shards_of).reshape((-1,) + (1,) * (len(shape) - 1 - position))
    return level


def normal_values(stream_key, dims, deviation, most, shards=(), kind=jnp.bfloat16):
    result = jax.random.normal(stream_key, dims, jnp.float32) * deviation
    if len(shards) > 0:
        result = shard_levels(stream_key, dims, shards, -0.22, 0.18) * result
    return jnp.clip(result, min=-most, max=most).astype(kind)


def setup_inputs(seed: int = 0) -> dict:
    seeds = jax.random.split(jax.random.key(seed), 6)
    return {
        "activations": draw_activations(jax.random.fold_in(seeds[5], 71), 0),
        "norm_gain": jnp.clip(1.0 + 0.15 * jax.random.normal(seeds[1], (D,), jnp.float32), 0.25, 1.75),
        "qkv_weight": draw_qkv_weight(jax.random.fold_in(seeds[5], 71), 0),
        "positions": draw_positions(jax.random.fold_in(seeds[5], 71), 0),
        "cotangent": normal_values(seeds[4], (TOKENS, HD), (TOKENS ** -0.5), 0.0625, ((0, 512),)),
    }


rope_base = 10000.0
norm_eps = 1e-05

def rope_tables(positions, head_size):
    half_width = head_size // 2
    exponent = jnp.arange(half_width, dtype=jnp.float32) * (-2.0 / head_size)
    frequency = jnp.power(jnp.float32(rope_base), exponent)
    angle_table = positions.astype(jnp.float32)[:, None] * frequency[None, :]
    angle_table = jnp.concatenate([angle_table, angle_table], axis=1)
    return (jnp.cos(angle_table), jnp.sin(angle_table))

def rotate(vectors, cosine_table, sine_table):
    half_width = vectors.shape[1] // 2
    turned = jnp.concatenate([-vectors[:, half_width:], vectors[:, :half_width]], axis=1)
    return vectors * cosine_table + turned * sine_table

def unrotate(gradient, cosine_table, sine_table):
    half_width = gradient.shape[1] // 2
    sined = gradient * sine_table
    turned = jnp.concatenate([sined[:, half_width:], -sined[:, :half_width]], axis=1)
    return gradient * cosine_table + turned

def normalize(activations, norm_gain):
    widened = activations.astype(jnp.float32)
    inverse_rms = lax.rsqrt(lax.optimization_barrier(jnp.mean(widened * widened, axis=1, keepdims=True)) + norm_eps)
    normed = (widened * inverse_rms * norm_gain[None, :]).astype(jnp.bfloat16)
    return (normed, inverse_rms, widened)

def attention_grads(projected, positions, cotangent):
    head_size = cotangent.shape[1]
    cosine_table, sine_table = rope_tables(positions, head_size)
    queries = rotate(projected[:, :head_size], cosine_table, sine_table).astype(jnp.bfloat16)
    keys_rot = rotate(projected[:, head_size:2 * head_size], cosine_table, sine_table).astype(jnp.bfloat16)
    values = projected[:, 2 * head_size:].astype(jnp.bfloat16)
    score_scale = head_size ** (-0.5)
    scores = lax.dot_general(queries, keys_rot, (((1,), (1,)), ((), ())), preferred_element_type=jnp.float32) * score_scale
    token_count = positions.shape[0]
    row_index = jnp.arange(token_count, dtype=jnp.int32)[:, None]
    column_index = jnp.arange(token_count, dtype=jnp.int32)[None, :]
    visible = (column_index <= row_index) & (row_index - column_index <= positions[:, None])
    scores = jnp.where(visible, scores, -jnp.inf)
    row_peak = lax.optimization_barrier(jnp.max(scores, axis=1, keepdims=True))
    exp_terms = jnp.exp(scores - row_peak)
    attention = exp_terms / lax.optimization_barrier(jnp.sum(exp_terms, axis=1, keepdims=True))
    attention_low = attention.astype(jnp.bfloat16)
    prob_grad = lax.dot_general(cotangent, values, (((1,), (1,)), ((), ())), preferred_element_type=jnp.float32)
    score_grad = (attention * (prob_grad - lax.optimization_barrier(jnp.sum(attention * prob_grad, axis=1, keepdims=True))) * score_scale).astype(jnp.bfloat16)
    query_grad = jnp.dot(score_grad, keys_rot, preferred_element_type=jnp.float32)
    key_grad = lax.dot_general(score_grad, queries, (((0,), (0,)), ((), ())), preferred_element_type=jnp.float32)
    value_grad = lax.dot_general(attention_low, cotangent, (((0,), (0,)), ((), ())), preferred_element_type=jnp.float32)
    joined = jnp.concatenate([unrotate(query_grad, cosine_table, sine_table), unrotate(key_grad, cosine_table, sine_table), value_grad], axis=1)
    return joined.astype(jnp.bfloat16)

def reference(activations, norm_gain, qkv_weight, positions, cotangent):
    block_count = activations.shape[0] // TOK_DEV
    act_blocks = activations.reshape(block_count, TOK_DEV, D)
    pos_blocks = positions.reshape(block_count, TOK_DEV)
    cot_blocks = cotangent.reshape(block_count, TOK_DEV, HD)

    def accumulate(running, block_items):
        block_act, block_pos, block_cot = block_items
        normed, inverse_rms, widened = normalize(block_act, norm_gain)
        projected = jnp.dot(normed, qkv_weight, preferred_element_type=jnp.float32)
        qkv_grads = attention_grads(projected, block_pos, block_cot)
        weight_term = lax.dot_general(normed, qkv_grads, (((0,), (0,)), ((), ())), preferred_element_type=jnp.float32)
        normed_grad = lax.dot_general(qkv_grads, qkv_weight, (((1,), (1,)), ((), ())), preferred_element_type=jnp.float32)
        gain_term = lax.optimization_barrier(jnp.sum(normed_grad * widened * inverse_rms, axis=0))
        return ((running[0] + weight_term, running[1] + gain_term), None)
    start_state = (jnp.zeros((D, 3 * HD), jnp.float32), jnp.zeros((D,), jnp.float32))
    (qkv_gradient, gain_gradient), _ = lax.scan(accumulate, start_state, (act_blocks, pos_blocks, cot_blocks))
    return (qkv_gradient, gain_gradient)
```

```python
import jax
import jax.numpy as jnp
from jax import lax
from jax.experimental import pallas as pl
from jax.sharding import Mesh, PartitionSpec as P

rope_base = 10000.0
norm_eps = 1e-05


def rope_tables(positions, head_size):
    half_width = head_size // 2
    exponent = jnp.arange(half_width, dtype=jnp.float32) * (-2.0 / head_size)
    frequency = jnp.power(jnp.float32(rope_base), exponent)
    angle_table = positions.astype(jnp.float32)[:, None] * frequency[None, :]
    angle_table = jnp.concatenate([angle_table, angle_table], axis=1)
    return (jnp.cos(angle_table), jnp.sin(angle_table))


def rotate(vectors, cosine_table, sine_table):
    half_width = vectors.shape[1] // 2
    turned = jnp.concatenate([-vectors[:, half_width:], vectors[:, :half_width]], axis=1)
    return vectors * cosine_table + turned * sine_table


def unrotate(gradient, cosine_table, sine_table):
    half_width = gradient.shape[1] // 2
    sined = gradient * sine_table
    turned = jnp.concatenate([sined[:, half_width:], -sined[:, :half_width]], axis=1)
    return gradient * cosine_table + turned


def normalize(activations, norm_gain):
    widened = activations.astype(jnp.float32)
    inverse_rms = lax.rsqrt(jnp.mean(widened * widened, axis=1, keepdims=True) + norm_eps)
    normed = (widened * inverse_rms * norm_gain[None, :]).astype(jnp.bfloat16)
    return (normed, inverse_rms, widened)


def attention_grads(projected, positions, cotangent):
    head_size = cotangent.shape[1]
    cosine_table, sine_table = rope_tables(positions, head_size)
    queries = rotate(projected[:, :head_size], cosine_table, sine_table).astype(jnp.bfloat16)
    keys_rot = rotate(projected[:, head_size : 2 * head_size], cosine_table, sine_table).astype(
        jnp.bfloat16
    )
    values = projected[:, 2 * head_size :].astype(jnp.bfloat16)
    score_scale = head_size ** (-0.5)
    scores = (
        lax.dot_general(
            queries, keys_rot, (((1,), (1,)), ((), ())), preferred_element_type=jnp.float32
        )
        * score_scale
    )
    token_count = positions.shape[0]
    row_index = jnp.arange(token_count, dtype=jnp.int32)[:, None]
    column_index = jnp.arange(token_count, dtype=jnp.int32)[None, :]
    visible = (column_index <= row_index) & (row_index - column_index <= positions[:, None])
    scores = jnp.where(visible, scores, -jnp.inf)
    row_peak = jnp.max(scores, axis=1, keepdims=True)
    exp_terms = jnp.exp(scores - row_peak)
    attention = exp_terms / jnp.sum(exp_terms, axis=1, keepdims=True)
    attention_low = attention.astype(jnp.bfloat16)
    prob_grad = lax.dot_general(
        cotangent, values, (((1,), (1,)), ((), ())), preferred_element_type=jnp.float32
    )
    score_grad = (
        attention
        * (prob_grad - jnp.sum(attention * prob_grad, axis=1, keepdims=True))
        * score_scale
    ).astype(jnp.bfloat16)
    query_grad = jnp.dot(score_grad, keys_rot, preferred_element_type=jnp.float32)
    key_grad = lax.dot_general(
        score_grad, queries, (((0,), (0,)), ((), ())), preferred_element_type=jnp.float32
    )
    value_grad = lax.dot_general(
        attention_low, cotangent, (((0,), (0,)), ((), ())), preferred_element_type=jnp.float32
    )
    joined = jnp.concatenate(
        [
            unrotate(query_grad, cosine_table, sine_table),
            unrotate(key_grad, cosine_table, sine_table),
            value_grad,
        ],
        axis=1,
    )
    return joined.astype(jnp.bfloat16)


AXES = ("y_hi", "x", "z", "y_lo", "core")
STEPS = 64.0
FULL = 32767.0


def broadcast_rows(block, count):
    rows, width = block.shape
    return jnp.broadcast_to(block[None], (count, rows, width)).reshape(count * rows, width)


def swap_cores(array):
    return lax.ppermute(array, "core", [(0, 1), (1, 0)])


def gather_plane(qkv_weight):
    width = qkv_weight.shape[1]
    member = lax.axis_index("y_hi") * 4 + lax.axis_index("x")
    part = lax.dynamic_slice(qkv_weight, (member * 8, 0), (8, width))
    along_z = lax.all_to_all(broadcast_rows(part, 16), "z", 0, 0, tiled=True)
    return lax.all_to_all(broadcast_rows(along_z, 16), ("y_hi", "x", "y_lo"), 0, 0, tiled=True)


def join_weight(own, other, core):
    width = own.shape[1]
    first = jnp.where(core == 0, own, other).reshape(8, 2, 16, 8, width)
    second = jnp.where(core == 0, other, own).reshape(8, 2, 16, 8, width)
    return jnp.stack([first, second]).transpose(3, 2, 0, 1, 4, 5).reshape(4096, width)


def split_exact(row):
    high = lax.reduce_precision(row, 8, 7)
    rest = row - high
    middle = lax.reduce_precision(rest, 8, 7)
    return jnp.concatenate([high, middle, rest - middle]).astype(jnp.bfloat16)


def redistribute(activations, inverse_rms, x_index, core):
    tokens = activations.shape[0]
    extra = split_exact(inverse_rms.reshape(1, tokens))
    extra = jnp.tile(jnp.pad(extra, ((0, 13), (0, 0))), (1, 4))[None]
    extra = jnp.concatenate([extra, extra])
    ordered = jnp.zeros((4, 2, tokens + 16, 512), jnp.bfloat16)
    for shift in range(4):
        column = lax.rem(x_index + shift, 4) * 512
        block = jnp.stack([lax.dynamic_slice(activations, (0, column + h * 2048), (tokens, 512)) for h in range(2)])
        block = jnp.concatenate([block, extra], axis=1)
        if shift:
            block = lax.ppermute(block, "x", [(i, (i + shift) % 4) for i in range(4)])
        ordered = lax.dynamic_update_slice(ordered, block[None], (lax.rem(x_index - shift + 4, 4), 0, 0, 0))
    first, second = ordered[..., :256], ordered[..., 256:]
    kept = jnp.where(core == 0, first, second)
    sent = jnp.where(core == 0, second, first)
    return kept, swap_cores(sent)


def scaled(block, gain_part):
    tokens = block.shape[2] - 16
    high, middle, low = (block[:, 0, tokens + k, :tokens].astype(jnp.float32) for k in range(3))
    inverse_rms = ((high + middle) + low)[:, None, :, None]
    unit = block[:, :, :tokens].astype(jnp.float32) * inverse_rms
    normed = (unit * gain_part.reshape(1, 2, 1, 256)).astype(jnp.bfloat16)
    return normed, unit


def code_kernel(parts_ref, coded_ref):
    sums = (parts_ref[0] + parts_ref[1]) + (parts_ref[2] + parts_ref[3])
    rows = sums[:, :64].reshape(16, 8, 384)
    gains = sums[:, 64:65, :128]
    peak = jnp.max(jnp.abs(rows), axis=1, keepdims=True)
    step = jnp.clip(jnp.ceil(jnp.log2(peak) * STEPS), -110 * STEPS, 127 * STEPS)
    coded = jnp.clip(jnp.round(rows * (jnp.exp2(step * (-1 / STEPS)) * FULL)), -FULL, FULL)
    gain_peak = jnp.max(jnp.abs(gains), axis=2, keepdims=True)
    gain_step = jnp.clip(jnp.ceil(jnp.log2(gain_peak) * STEPS), -110 * STEPS, 127 * STEPS)
    scaled_gains = gains * (jnp.exp2(gain_step * (-1 / STEPS)) * FULL)
    high = jnp.clip(jnp.round(scaled_gains), -FULL, FULL)
    low = jnp.clip(jnp.round((scaled_gains - high) * FULL), -FULL, FULL)
    shown = [jnp.broadcast_to(v[:, None], (2, 8, 1, 128)).reshape(16, 1, 128) for v in (high, low, jnp.broadcast_to(gain_step, (2, 1, 128)))]
    extra = jnp.concatenate(
        [step[:, :, :128], step[:, :, 128:256], step[:, :, 256:]] + shown + [jnp.zeros((16, 2, 128), jnp.float32)], axis=1
    )
    whole = jnp.concatenate([coded, extra], axis=2).reshape(128, 512)
    coded_ref[...] = whole.astype(jnp.int32).astype(jnp.int16)


def decode_kernel(coded_ref, rows_ref, gains_ref):
    whole = coded_ref[...].astype(jnp.int32).astype(jnp.float32).reshape(16, 8, 512)
    extra = whole[:, :, 384:]
    step = jnp.concatenate([extra[:, 0:1], extra[:, 1:2], extra[:, 2:3]], axis=2)
    rows_ref[...] = jnp.sum(whole[:, :, :384] * (jnp.exp2(step * (1 / STEPS)) * (1 / FULL)), axis=0)
    scale = jnp.exp2(extra[:, 5:6] * (1 / STEPS)) * (1 / FULL)
    gains_ref[...] = jnp.sum((extra[:, 3:4] + extra[:, 4:5] * (1 / FULL)) * scale, axis=0)


def shards(activations, norm_gain, qkv_weight, positions, cotangent):
    x_index = lax.axis_index("x")
    core = lax.axis_index("core")
    width = qkv_weight.shape[1]
    tokens = activations.shape[0]
    normed, inverse_rms, _ = normalize(activations, norm_gain)
    own_weight = gather_plane(qkv_weight)
    kept, received = redistribute(activations, inverse_rms, x_index, core)
    gain_part = lax.dynamic_slice(norm_gain.reshape(2, 8, 256), (0, x_index * 2 + core, 0), (2, 1, 256)).reshape(512)
    kept = scaled(kept, gain_part)
    received = scaled(received, gain_part)
    own_weight, normed, kept, received = lax.optimization_barrier((own_weight, normed, kept, received))

    weight = join_weight(own_weight, swap_cores(own_weight), core)
    projected = jnp.dot(normed, weight, preferred_element_type=jnp.float32)
    qkv_grads = attention_grads(projected, positions, cotangent)
    weight_rows = lax.dynamic_slice(weight.reshape(2, 8, 256, width), (0, x_index * 2 + core, 0, 0), (2, 1, 256, width)).reshape(2, 256, width)

    own_grads = lax.all_to_all(broadcast_rows(qkv_grads, 4), "x", 0, 0, tiled=True)
    other_grads = swap_cores(own_grads)

    weight_term, gain_term = 0.0, 0.0
    for (block_normed, block_unit), grads in ((kept, own_grads), (received, other_grads)):
        grads = grads.reshape(4, tokens, width)
        weight_term += jnp.einsum("xhtd,xtj->hdj", block_normed, grads, preferred_element_type=jnp.float32)
        normed_grad = jnp.einsum("xtj,hdj->xhtd", grads, weight_rows, preferred_element_type=jnp.float32)
        gain_term += jnp.sum(normed_grad * block_unit, axis=(0, 2))

    parts = weight_term.reshape(2, 8, 2, 2, 8, width).transpose(0, 2, 3, 1, 4, 5).reshape(8, 64, width)
    gains = gain_term.reshape(2, 8, 2, 2, 8).transpose(0, 2, 3, 1, 4).reshape(8, 1, 64)
    parts = jnp.concatenate([parts, jnp.pad(gains, ((0, 0), (0, 7), (0, width - 64)))], axis=1)
    parts = lax.all_to_all(parts, ("y_hi", "y_lo", "core"), 0, 0, tiled=True)
    coded = pl.pallas_call(
        code_kernel, out_shape=jax.ShapeDtypeStruct((128, 512), jnp.int16), name="code_rows"
    )(parts.reshape(4, 2, 72, width))
    coded = lax.all_to_all(coded, "z", 0, 0, tiled=True)
    share, gains = pl.pallas_call(
        decode_kernel,
        out_shape=(jax.ShapeDtypeStruct((8, width), jnp.float32), jax.ShapeDtypeStruct((1, 128), jnp.float32)),
        name="decode_rows",
    )(coded)
    place = lax.rem(lax.axis_index("z"), 8) * 8
    return share, lax.dynamic_slice(gains, (0, place), (1, 8)).reshape(8)


def solution(mesh):
    fine = Mesh(mesh.devices.reshape(2, 4, 16, 2, 2), AXES)
    placed = (
        P(AXES, None),
        P(),
        P(("z", "y_lo", "core"), None),
        P(AXES),
        P(AXES, None),
    )
    return jax.shard_map(
        shards,
        mesh=fine,
        in_specs=placed,
        out_specs=(P(AXES, None), P(AXES)),
        check_vma=False,
    )
```

```python
import jax
import jax.numpy as jnp
from jax import lax
from jax.experimental import pallas as pl
from jax.experimental.pallas import tpu as pltpu
from jax.sharding import Mesh, PartitionSpec as P

rope_base = 10000.0
norm_eps = 1e-05


def rope_tables(positions, head_size):
    half_width = head_size // 2
    exponent = jnp.arange(half_width, dtype=jnp.float32) * (-2.0 / head_size)
    frequency = jnp.power(jnp.float32(rope_base), exponent)
    angle_table = positions.astype(jnp.float32)[:, None] * frequency[None, :]
    angle_table = jnp.concatenate([angle_table, angle_table], axis=1)
    return (jnp.cos(angle_table), jnp.sin(angle_table))


def rotate(vectors, cosine_table, sine_table):
    half_width = vectors.shape[1] // 2
    turned = jnp.concatenate([-vectors[:, half_width:], vectors[:, :half_width]], axis=1)
    return vectors * cosine_table + turned * sine_table


def unrotate(gradient, cosine_table, sine_table):
    half_width = gradient.shape[1] // 2
    sined = gradient * sine_table
    turned = jnp.concatenate([sined[:, half_width:], -sined[:, :half_width]], axis=1)
    return gradient * cosine_table + turned


def normalize(activations, norm_gain):
    widened = activations.astype(jnp.float32)
    inverse_rms = lax.rsqrt(jnp.mean(widened * widened, axis=1, keepdims=True) + norm_eps)
    normed = (widened * inverse_rms * norm_gain[None, :]).astype(jnp.bfloat16)
    return (normed, inverse_rms, widened)


def attention_grads(projected, positions, cotangent):
    head_size = cotangent.shape[1]
    cosine_table, sine_table = rope_tables(positions, head_size)
    queries = rotate(projected[:, :head_size], cosine_table, sine_table).astype(jnp.bfloat16)
    keys_rot = rotate(projected[:, head_size : 2 * head_size], cosine_table, sine_table).astype(
        jnp.bfloat16
    )
    values = projected[:, 2 * head_size :].astype(jnp.bfloat16)
    score_scale = head_size ** (-0.5)
    scores = (
        lax.dot_general(
            queries, keys_rot, (((1,), (1,)), ((), ())), preferred_element_type=jnp.float32
        )
        * score_scale
    )
    token_count = positions.shape[0]
    row_index = jnp.arange(token_count, dtype=jnp.int32)[:, None]
    column_index = jnp.arange(token_count, dtype=jnp.int32)[None, :]
    visible = (column_index <= row_index) & (row_index - column_index <= positions[:, None])
    scores = jnp.where(visible, scores, -jnp.inf)
    row_peak = jnp.max(scores, axis=1, keepdims=True)
    exp_terms = jnp.exp(scores - row_peak)
    attention = exp_terms / jnp.sum(exp_terms, axis=1, keepdims=True)
    attention_low = attention.astype(jnp.bfloat16)
    prob_grad = lax.dot_general(
        cotangent, values, (((1,), (1,)), ((), ())), preferred_element_type=jnp.float32
    )
    score_grad = (
        attention
        * (prob_grad - jnp.sum(attention * prob_grad, axis=1, keepdims=True))
        * score_scale
    ).astype(jnp.bfloat16)
    query_grad = jnp.dot(score_grad, keys_rot, preferred_element_type=jnp.float32)
    key_grad = lax.dot_general(
        score_grad, queries, (((0,), (0,)), ((), ())), preferred_element_type=jnp.float32
    )
    value_grad = lax.dot_general(
        attention_low, cotangent, (((0,), (0,)), ((), ())), preferred_element_type=jnp.float32
    )
    joined = jnp.concatenate(
        [
            unrotate(query_grad, cosine_table, sine_table),
            unrotate(key_grad, cosine_table, sine_table),
            value_grad,
        ],
        axis=1,
    )
    return joined.astype(jnp.bfloat16)


AXES = ("y_hi", "x", "z", "y_lo", "core")
STEPS = 64.0
SMALL = pltpu.CompilerParams(vmem_limit_bytes=8 * 2**20)
FULL = 32767.0


def broadcast_rows(block, count):
    rows, width = block.shape
    return jnp.broadcast_to(block[None], (count, rows, width)).reshape(count * rows, width)


def swap_cores(array):
    return lax.ppermute(array, "core", [(0, 1), (1, 0)])


def gather_plane(qkv_weight):
    width = qkv_weight.shape[1]
    member = lax.axis_index("y_hi") * 4 + lax.axis_index("x")
    part = lax.dynamic_slice(qkv_weight, (member * 8, 0), (8, width))
    along_z = lax.all_to_all(broadcast_rows(part, 16), "z", 0, 0, tiled=True)
    return along_z, lax.all_to_all(broadcast_rows(along_z, 16), ("y_hi", "x", "y_lo"), 0, 0, tiled=True)


def join_weight(own, core):
    width = own.shape[1]
    other = swap_cores(own)
    weight = jnp.zeros((16, 2, 2, 8, 8, width), own.dtype)
    for block, side in ((own, core), (other, 1 - core)):
        block = block.reshape(8, 2, 16, 8, width).transpose(2, 1, 0, 3, 4)
        weight = lax.dynamic_update_slice(weight, block[:, :, None], (0, 0, side, 0, 0, 0))
    return weight.reshape(4096, width)


def split_exact(row):
    high = lax.reduce_precision(row, 8, 7)
    rest = row - high
    middle = lax.reduce_precision(rest, 8, 7)
    return jnp.concatenate([high, middle, rest - middle]).astype(jnp.bfloat16)


def redistribute(activations, inverse_rms, x_index, core, after):
    tokens = activations.shape[0]
    extra = split_exact(inverse_rms.reshape(1, tokens))
    extra = jnp.tile(jnp.pad(extra, ((0, 13), (0, 0))), (1, 4))[None]
    extra = jnp.concatenate([extra, extra])
    blocks = []
    for shift in range(4):
        column = lax.rem(x_index + shift, 4) * 512
        block = jnp.stack([lax.dynamic_slice(activations, (0, column + h * 2048), (tokens, 512)) for h in range(2)])
        block = jnp.concatenate([block, extra], axis=1)
        if shift:
            block = lax.ppermute(block, "x", [(i, (i + shift) % 4) for i in range(4)])
        blocks.append(block)
    ordered = jnp.broadcast_to(after[:1, :1].reshape(1, 1, 1, 1), (4, 2, tokens + 16, 512))
    for shift, block in enumerate(blocks):
        ordered = lax.dynamic_update_slice(ordered, block[None], (lax.rem(x_index - shift + 4, 4), 0, 0, 0))
    first, second = ordered[..., :256], ordered[..., 256:]
    kept = jnp.where(core == 0, first, second)
    sent = jnp.where(core == 0, second, first)
    return kept, swap_cores(sent)


def prepare_kernel(block_ref, gain_ref, normed_ref, unit_ref):
    for x in range(4):
        for half in range(2):
            block = block_ref[x, half].astype(jnp.float32)
            inverse_rms = (block[128:129, :128] + block[129:130, :128]) + block[130:131, :128]
            unit = block[:128].T * inverse_rms
            place = (pl.ds(half * 256, 256), pl.ds(x * 128, 128))
            unit_ref[place] = unit
            normed_ref[place] = (unit * gain_ref[pl.ds(half * 256, 256), :]).astype(jnp.bfloat16)


def prepared(block, gain_part):
    return pl.pallas_call(
        prepare_kernel,
        out_shape=(jax.ShapeDtypeStruct((512, 512), jnp.bfloat16), jax.ShapeDtypeStruct((512, 512), jnp.float32)),
        name="prepare_columns",
        compiler_params=pltpu.CompilerParams(vmem_limit_bytes=16 * 2**20),
    )(block, gain_part.reshape(512, 1))


def step_of(values, axis):
    peak = jnp.max(jnp.abs(values), axis=axis, keepdims=True)
    return jnp.clip(jnp.ceil(jnp.log2(peak) * STEPS), -110 * STEPS, 127 * STEPS)


def coded_values(values, step):
    return jnp.clip(jnp.round(values * (jnp.exp2(step * (-1 / STEPS)) * FULL)), -FULL, FULL)


def decoded_scale(step):
    return jnp.exp2(step * (1 / STEPS)) * (1 / FULL)


def coded_gain(gains):
    step = step_of(gains, -1)
    exact = gains * (jnp.exp2(step * (-1 / STEPS)) * FULL)
    high = jnp.clip(jnp.round(exact), -FULL, FULL)
    low = jnp.clip(jnp.round((exact - high) * FULL), -FULL, FULL)
    return high, low, jnp.broadcast_to(step, gains.shape)


def narrow(values):
    return values.astype(jnp.int32).astype(jnp.int16)


def wide(codes):
    return codes.astype(jnp.int32).astype(jnp.float32)


def grads_kernel(kept_ref, kept_unit_ref, received_ref, received_unit_ref, own_ref, other_ref, rows_ref, coded_ref, term_ref):
    term_ref[...] = jnp.dot(kept_ref[...], own_ref[...], preferred_element_type=jnp.float32) + jnp.dot(
        received_ref[...], other_ref[...], preferred_element_type=jnp.float32
    )
    gain = 0.0
    for unit_ref, grads_ref in ((kept_unit_ref, own_ref), (received_unit_ref, other_ref)):
        normed_grad = lax.dot_general(
            rows_ref[...], grads_ref[...], (((1,), (1,)), ((), ())), preferred_element_type=jnp.float32
        )
        gain += jnp.sum(normed_grad * unit_ref[...], axis=1, keepdims=True)
    lanes = lax.broadcasted_iota(jnp.int32, (64, 128), 1)
    table = jnp.zeros((64, 128), jnp.float32)
    for chunk in range(8):
        first = chunk // 4 * 256 + chunk % 4 * 8
        column = jnp.concatenate([gain[first + z * 32 : first + z * 32 + 8] for z in range(8)])
        table = jnp.where(lanes == chunk, column, table)
    table = jnp.concatenate([table, jnp.zeros((64, 128), jnp.float32)]).T
    gains = coded_gain(table[:8])
    for chunk in range(8):
        first = chunk // 4 * 256 + chunk % 4 * 8
        rows = jnp.concatenate([term_ref[pl.ds(first + z * 32, 8), :] for z in range(8)])
        step = step_of(rows, 0)
        shown = [jnp.pad(part[chunk : chunk + 1], ((0, 0), (0, 256))) for part in gains]
        whole = [coded_values(rows, step), step] + shown + [jnp.zeros((4, 384), jnp.float32)]
        coded_ref[chunk] = narrow(jnp.concatenate(whole))


def code_z_kernel(parts_ref, coded_ref):
    rows, gains = [], []
    for core in range(2):
        row_sum, gain_sum = 0.0, 0.0
        for y in range(4):
            part = wide(parts_ref[y * 2 + core])
            extra = part[64:]
            row_sum += part[:64] * decoded_scale(extra[0:1])
            gain_sum += (extra[1:2, :128] + extra[2:3, :128] * (1 / FULL)) * decoded_scale(extra[3:4, :128])
        rows.append(row_sum)
        gains.append(gain_sum)
    rows = jnp.concatenate(rows).reshape(16, 8, 384)
    step = step_of(rows, 1)
    shown = jnp.concatenate(coded_gain(jnp.concatenate(gains)) + (jnp.zeros((2, 128), jnp.float32),))
    extra = []
    for z in range(16):
        moved = shown if z % 8 == 0 else pltpu.roll(shown, 128 - z % 8 * 8, 1)
        core = z // 8
        extra.append(jnp.concatenate(
            [step[z, :, k * 128 : (k + 1) * 128] for k in range(3)]
            + [moved[k + core : k + core + 1] for k in (0, 2, 4)]
            + [jnp.zeros((2, 128), jnp.float32)]
        ))
    whole = jnp.concatenate([coded_values(rows, step).reshape(128, 384), jnp.concatenate(extra)], axis=1)
    coded_ref[...] = narrow(whole)


def decode_kernel(coded_ref, rows_ref, gains_ref):
    whole = wide(coded_ref[...]).reshape(16, 8, 512)
    extra = whole[:, :, 384:]
    step = jnp.concatenate([extra[:, 0:1], extra[:, 1:2], extra[:, 2:3]], axis=2)
    rows_ref[...] = jnp.sum(whole[:, :, :384] * decoded_scale(step), axis=0)
    gains = (extra[:, 3:4] + extra[:, 4:5] * (1 / FULL)) * decoded_scale(extra[:, 5:6])
    gains_ref[...] = jnp.sum(gains, axis=0)[:, :8]


def shards(activations, norm_gain, qkv_weight, positions, cotangent):
    x_index = lax.axis_index("x")
    core = lax.axis_index("core")
    width = qkv_weight.shape[1]
    tokens = activations.shape[0]
    normed, inverse_rms, _ = normalize(activations, norm_gain)
    along_z, own_weight = gather_plane(qkv_weight)
    kept, received = redistribute(activations, inverse_rms, x_index, core, along_z)
    gain_part = lax.dynamic_slice(norm_gain.reshape(2, 8, 256), (0, x_index * 2 + core, 0), (2, 1, 256)).reshape(512)
    kept = prepared(kept, gain_part)
    received = prepared(received, gain_part)
    own_weight, normed, kept, received = lax.optimization_barrier((own_weight, normed, kept, received))

    weight = join_weight(own_weight, core)
    projected = jnp.dot(normed, weight, preferred_element_type=jnp.float32)
    qkv_grads = attention_grads(projected, positions, cotangent)
    weight_rows = lax.dynamic_slice(weight.reshape(2, 8, 256, width), (0, x_index * 2 + core, 0, 0), (2, 1, 256, width)).reshape(512, width)

    own_grads = lax.all_to_all(broadcast_rows(qkv_grads, 4), "x", 0, 0, tiled=True)
    other_grads = swap_cores(own_grads)

    parts = pl.pallas_call(
        grads_kernel,
        out_shape=jax.ShapeDtypeStruct((8, 72, width), jnp.int16),
        scratch_shapes=[pltpu.VMEM((512, width), jnp.float32)],
        name="code_y",
        compiler_params=pltpu.CompilerParams(vmem_limit_bytes=16 * 2**20),
    )(*kept, *received, own_grads, other_grads, weight_rows)
    parts = lax.all_to_all(parts, ("y_hi", "y_lo", "core"), 0, 0, tiled=True)
    coded = pl.pallas_call(
        code_z_kernel, out_shape=jax.ShapeDtypeStruct((128, 512), jnp.int16), name="code_z", compiler_params=SMALL
    )(parts)
    coded = lax.all_to_all(coded, "z", 0, 0, tiled=True)
    share, gains = pl.pallas_call(
        decode_kernel,
        out_shape=(jax.ShapeDtypeStruct((8, width), jnp.float32), jax.ShapeDtypeStruct((1, 8), jnp.float32)),
        name="decode_rows", compiler_params=SMALL,
    )(coded)
    return share, gains.reshape(8)


def solution(mesh):
    fine = Mesh(mesh.devices.reshape(2, 4, 16, 2, 2), AXES)
    placed = (
        P(AXES, None),
        P(),
        P(("z", "y_lo", "core"), None),
        P(AXES),
        P(AXES, None),
    )
    return jax.shard_map(
        shards,
        mesh=fine,
        in_specs=placed,
        out_specs=(P(AXES, None), P(AXES)),
        check_vma=False,
    )
```

```python
import jax
import jax.numpy as jnp
from jax import lax
from jax.experimental import pallas as pl
from jax.experimental.pallas import tpu as pltpu
from jax.sharding import Mesh, PartitionSpec as P

rope_base = 10000.0
norm_eps = 1e-05


def angle_kernel(positions_ref, frequency_ref, after_ref, angles_ref):
    angles_ref[...] = positions_ref[...].astype(jnp.float32) * frequency_ref[...]


def rope_tables(positions, head_size, after):
    half_width = head_size // 2
    exponent = jnp.arange(half_width, dtype=jnp.float32) * (-2.0 / head_size)
    frequency = jnp.power(jnp.float32(rope_base), exponent)
    frequency = jnp.concatenate([frequency, frequency])[None]
    vmem = pl.BlockSpec(memory_space=pltpu.VMEM)
    angle_table = pl.pallas_call(
        angle_kernel,
        out_shape=jax.ShapeDtypeStruct((positions.shape[0], head_size), jnp.float32),
        in_specs=[vmem, vmem, pl.BlockSpec(memory_space=pl.ANY)],
        out_specs=vmem,
        name="angles",
        compiler_params=SMALL,
        cost_estimate=BRIEF,
    )(positions, frequency, after)
    return (jnp.cos(angle_table), jnp.sin(angle_table))


def normalize(activations, norm_gain):
    widened = activations.astype(jnp.float32)
    inverse_rms = lax.rsqrt(jnp.mean(widened * widened, axis=1, keepdims=True) + norm_eps)
    return (widened * inverse_rms * norm_gain[None, :]).astype(jnp.bfloat16)


def attention_kernel(
    core_ref, own_ref, other_ref, normed_ref, cosine_ref, sine_ref, positions_ref, cotangent_ref, grads_ref, rows_ref, weight_ref
):
    projected = project(core_ref, own_ref, other_ref, normed_ref, weight_ref, rows_ref)
    cosine, sine = cosine_ref[...], sine_ref[...]
    lower = lax.broadcasted_iota(jnp.int32, (128, 128), 1) < 64
    turned_sine = jnp.where(lower, -sine, sine)

    def rotate(part):
        return (part * cosine + pltpu.roll(part, 64, 1) * turned_sine).astype(jnp.bfloat16)

    def unrotate(part):
        return part * cosine + pltpu.roll(part * turned_sine, 64, 1)

    def product(left, right, over):
        return lax.dot_general(left, right, (((over[0],), (over[1],)), ((), ())), preferred_element_type=jnp.float32)

    queries, keys_rot = rotate(projected[:, :128]), rotate(projected[:, 128:256])
    values = projected[:, 256:].astype(jnp.bfloat16)
    cotangent = cotangent_ref[...]
    score_scale = 128 ** (-0.5)
    scores = product(queries, keys_rot, (1, 1)) * score_scale
    row_index = lax.broadcasted_iota(jnp.int32, (128, 128), 0)
    column_index = lax.broadcasted_iota(jnp.int32, (128, 128), 1)
    visible = (column_index <= row_index) & (row_index - column_index <= positions_ref[...])
    scores = jnp.where(visible, scores, -jnp.inf)
    exp_terms = jnp.exp(scores - jnp.max(scores, axis=1, keepdims=True))
    attention = exp_terms / jnp.sum(exp_terms, axis=1, keepdims=True)
    attention_low = attention.astype(jnp.bfloat16)
    prob_grad = product(cotangent, values, (1, 1))
    score_grad = (
        attention * (prob_grad - jnp.sum(attention * prob_grad, axis=1, keepdims=True)) * score_scale
    ).astype(jnp.bfloat16)
    grads = jnp.concatenate(
        [
            unrotate(product(score_grad, keys_rot, (1, 0))),
            unrotate(product(score_grad, queries, (0, 0))),
            product(attention_low, cotangent, (0, 0)),
        ],
        axis=1,
    ).astype(jnp.bfloat16)
    for copy in range(4):
        grads_ref[copy] = grads


def attention_grads(place, own, normed, tables, positions, cotangent):
    tokens, width = normed.shape[0], own.shape[1]
    raw = own.reshape(8, 2, 16, 8, width)
    ordered = pl.pallas_call(
        order_kernel,
        out_shape=jax.ShapeDtypeStruct((16, 2, 64, width), own.dtype),
        name="order_rows",
        compiler_params=SMALL,
        cost_estimate=BRIEF,
    )(raw)
    vmem = pl.BlockSpec(memory_space=pltpu.VMEM)
    grads, rows = pl.pallas_call(
        attention_kernel,
        out_shape=(
            jax.ShapeDtypeStruct((4, tokens, width), jnp.bfloat16),
            jax.ShapeDtypeStruct((512, width), jnp.bfloat16),
        ),
        in_specs=[pl.BlockSpec(memory_space=pltpu.SMEM)] + [vmem] * 7,
        out_specs=(vmem, vmem),
        scratch_shapes=[pltpu.VMEM((4096, width), jnp.bfloat16)],
        name="attention_grads",
        compiler_params=pltpu.CompilerParams(vmem_limit_bytes=20 * 2**20),
    )(place, ordered, swap_cores(own).reshape(raw.shape), normed, *tables, positions, cotangent)
    return grads.reshape(4 * tokens, width), rows


AXES = ("y_hi", "x", "z", "y_lo", "core")
STEPS = 64.0
BRIEF = pl.CostEstimate(flops=2**20, bytes_accessed=2**18, transcendentals=0)
SMALL = pltpu.CompilerParams(vmem_limit_bytes=8 * 2**20)
FULL = 32767.0


def broadcast_rows(block, count):
    rows, width = block.shape
    return jnp.broadcast_to(block[None], (count, rows, width)).reshape(count * rows, width)


def swap_cores(array):
    return lax.ppermute(array, "core", [(0, 1), (1, 0)])


def copy_kernel(part_ref, copies_ref, seed_ref):
    for copy in range(16):
        copies_ref[copy] = part_ref[...]
    seed_ref[...] = jnp.zeros_like(seed_ref)


def gather_plane(qkv_weight):
    width = qkv_weight.shape[1]
    member = lax.axis_index("y_hi") * 4 + lax.axis_index("x")
    part = lax.dynamic_slice(qkv_weight, (member * 8, 0), (8, width))
    along_z = lax.all_to_all(broadcast_rows(part, 16), "z", 0, 0, tiled=True)
    copies, seed = pl.pallas_call(
        copy_kernel,
        out_shape=(jax.ShapeDtypeStruct((16, 128, width), jnp.bfloat16), jax.ShapeDtypeStruct((1, 512), jnp.bfloat16)),
        name="copy_rows",
        compiler_params=SMALL,
    )(along_z)
    plane = lax.all_to_all(copies.reshape(2048, width), ("y_hi", "x", "y_lo"), 0, 0, tiled=True)
    return seed, plane


def order_kernel(raw_ref, ordered_ref):
    for z in range(16):
        for y in range(2):
            rows = [raw_ref[eighth, y, z].astype(jnp.float32) for eighth in range(8)]
            ordered_ref[z, y] = jnp.concatenate(rows).astype(jnp.bfloat16)


def project(core_ref, own_ref, other_ref, normed_ref, weight_ref, rows_ref):
    core, column = core_ref[0], core_ref[1]
    for z in range(16):
        for y in range(2):
            rows = [other_ref[eighth, y, z].astype(jnp.float32) for eighth in range(8)]
            place = z * 256 + y * 128
            weight_ref[pl.ds(pl.multiple_of(place + core * 64, 64), 64), :] = own_ref[z, y]
            weight_ref[pl.ds(pl.multiple_of(place + (1 - core) * 64, 64), 64), :] = jnp.concatenate(rows).astype(jnp.bfloat16)
    for half in range(2):
        start = pl.multiple_of(half * 2048 + column * 256, 256)
        rows_ref[pl.ds(half * 256, 256), :] = weight_ref[pl.ds(start, 256), :]
    return jnp.dot(normed_ref[...], weight_ref[...], preferred_element_type=jnp.float32)


def blocks_kernel(x_ref, activations_ref, *block_refs):
    squares = 0.0
    for part in range(4):
        widened = activations_ref[:, part * 1024 : (part + 1) * 1024].astype(jnp.float32)
        squares += jnp.sum(widened * widened, axis=1, keepdims=True)
    inverse_rms = jnp.broadcast_to(lax.rsqrt(squares / 4096 + norm_eps), (128, 128)).T
    high = inverse_rms.astype(jnp.bfloat16).astype(jnp.float32)
    rest = inverse_rms - high
    middle = rest.astype(jnp.bfloat16).astype(jnp.float32)
    row = lax.broadcasted_iota(jnp.int32, (128, 128), 0)
    extra = jnp.where(row == 0, high, jnp.where(row == 1, middle, jnp.where(row == 2, rest - middle, 0.0)))
    extra = jnp.concatenate([extra[:16]] * 4, axis=1).astype(jnp.bfloat16)
    for shift, block_ref in enumerate(block_refs):
        target = lax.rem(x_ref[0] + shift, 4)
        for half in range(2):
            start = pl.multiple_of(half * 2048 + target * 512, 512)
            block_ref[half, pl.ds(0, 128), :] = activations_ref[:, pl.ds(start, 512)]
            block_ref[half, pl.ds(128, 16), :] = extra


def redistribute(activations, x_index, core, seed):
    tokens = activations.shape[0]
    vmem = pl.BlockSpec(memory_space=pltpu.VMEM)
    blocks = pl.pallas_call(
        blocks_kernel,
        out_shape=[jax.ShapeDtypeStruct((2, tokens + 16, 512), jnp.bfloat16)] * 4,
        in_specs=[pl.BlockSpec(memory_space=pltpu.SMEM), vmem],
        out_specs=[vmem] * 4,
        name="cut_blocks",
        compiler_params=SMALL,
        cost_estimate=BRIEF,
    )(x_index.reshape(1), activations)
    ordered = jnp.broadcast_to(seed.reshape(1, 1, 1, 512), (4, 2, tokens + 16, 512))
    for shift, block in enumerate(blocks):
        if shift:
            block = lax.ppermute(block, "x", [(i, (i + shift) % 4) for i in range(4)])
        ordered = lax.dynamic_update_slice(ordered, block[None], (lax.rem(x_index - shift + 4, 4), 0, 0, 0))
    first, second = ordered[..., :256], ordered[..., 256:]
    kept = jnp.where(core == 0, first, second)
    sent = jnp.where(core == 0, second, first)
    return kept, swap_cores(sent)


def prepare_kernel(block_ref, gain_ref, normed_ref, unit_ref):
    for x in range(4):
        for half in range(2):
            block = block_ref[x, half].astype(jnp.float32)
            inverse_rms = (block[128:129, :128] + block[129:130, :128]) + block[130:131, :128]
            unit = block[:128].T * inverse_rms
            place = (pl.ds(half * 256, 256), pl.ds(x * 128, 128))
            unit_ref[place] = unit
            normed_ref[place] = (unit * gain_ref[pl.ds(half * 256, 256), :]).astype(jnp.bfloat16)


def prepared(block, gain_part):
    return pl.pallas_call(
        prepare_kernel,
        out_shape=(jax.ShapeDtypeStruct((512, 512), jnp.bfloat16), jax.ShapeDtypeStruct((512, 512), jnp.float32)),
        name="prepare_columns",
        compiler_params=pltpu.CompilerParams(vmem_limit_bytes=16 * 2**20),
    )(block, gain_part.reshape(512, 1))


def step_of(values, axis):
    peak = jnp.max(jnp.abs(values), axis=axis, keepdims=True)
    return jnp.clip(jnp.ceil(jnp.log2(peak) * STEPS), -110 * STEPS, 127 * STEPS)


def coded_values(values, step):
    return jnp.clip(jnp.round(values * (jnp.exp2(step * (-1 / STEPS)) * FULL)), -FULL, FULL)


def decoded_scale(step):
    return jnp.exp2(step * (1 / STEPS)) * (1 / FULL)


def coded_gain(gains):
    step = step_of(gains, -1)
    exact = gains * (jnp.exp2(step * (-1 / STEPS)) * FULL)
    high = jnp.clip(jnp.round(exact), -FULL, FULL)
    low = jnp.clip(jnp.round((exact - high) * FULL), -FULL, FULL)
    return high, low, jnp.broadcast_to(step, gains.shape)


def narrow(values):
    return values.astype(jnp.int32).astype(jnp.int16)


def wide(codes):
    return codes.astype(jnp.int32).astype(jnp.float32)


def half_grads(normed_ref, unit_ref, grads_ref, rows_ref):
    term = jnp.dot(normed_ref[...], grads_ref[...], preferred_element_type=jnp.float32)
    normed_grad = lax.dot_general(
        rows_ref[...], grads_ref[...], (((1,), (1,)), ((), ())), preferred_element_type=jnp.float32
    )
    return term, jnp.sum(normed_grad * unit_ref[...], axis=1, keepdims=True)


def first_grads_kernel(normed_ref, unit_ref, grads_ref, rows_ref, term_ref, gain_ref):
    term_ref[...], gain_ref[...] = half_grads(normed_ref, unit_ref, grads_ref, rows_ref)


def grads_kernel(first_ref, first_gain_ref, normed_ref, unit_ref, grads_ref, rows_ref, coded_ref, term_ref):
    term, gain = half_grads(normed_ref, unit_ref, grads_ref, rows_ref)
    term_ref[...] = first_ref[...] + term
    gain = first_gain_ref[...] + gain
    lanes = lax.broadcasted_iota(jnp.int32, (64, 128), 1)
    table = jnp.zeros((64, 128), jnp.float32)
    for chunk in range(8):
        first = chunk // 4 * 256 + chunk % 4 * 8
        column = jnp.concatenate([gain[first + z * 32 : first + z * 32 + 8] for z in range(8)])
        table = jnp.where(lanes == chunk, column, table)
    table = jnp.concatenate([table, jnp.zeros((64, 128), jnp.float32)]).T
    gains = coded_gain(table[:8])
    for chunk in range(8):
        first = chunk // 4 * 256 + chunk % 4 * 8
        rows = jnp.concatenate([term_ref[pl.ds(first + z * 32, 8), :] for z in range(8)])
        step = step_of(rows, 0)
        shown = [jnp.pad(part[chunk : chunk + 1], ((0, 0), (0, 256))) for part in gains]
        whole = [coded_values(rows, step), step] + shown + [jnp.zeros((4, 384), jnp.float32)]
        coded_ref[chunk] = narrow(jnp.concatenate(whole))


def code_z_kernel(parts_ref, coded_ref):
    rows, gains = [], []
    for core in range(2):
        row_sum, gain_sum = 0.0, 0.0
        for y in range(4):
            part = wide(parts_ref[y * 2 + core])
            extra = part[64:]
            row_sum += part[:64] * decoded_scale(extra[0:1])
            gain_sum += (extra[1:2, :128] + extra[2:3, :128] * (1 / FULL)) * decoded_scale(extra[3:4, :128])
        rows.append(row_sum)
        gains.append(gain_sum)
    rows = jnp.concatenate(rows).reshape(16, 8, 384)
    step = step_of(rows, 1)
    shown = jnp.concatenate(coded_gain(jnp.concatenate(gains)) + (jnp.zeros((2, 128), jnp.float32),))
    extra = []
    for z in range(16):
        moved = shown if z % 8 == 0 else pltpu.roll(shown, 128 - z % 8 * 8, 1)
        core = z // 8
        extra.append(jnp.concatenate(
            [step[z, :, k * 128 : (k + 1) * 128] for k in range(3)]
            + [moved[k + core : k + core + 1] for k in (0, 2, 4)]
            + [jnp.zeros((2, 128), jnp.float32)]
        ))
    whole = jnp.concatenate([coded_values(rows, step).reshape(128, 384), jnp.concatenate(extra)], axis=1)
    coded_ref[...] = narrow(whole)


def decode_kernel(coded_ref, rows_ref, gains_ref):
    whole = wide(coded_ref[...]).reshape(16, 8, 512)
    extra = whole[:, :, 384:]
    step = jnp.concatenate([extra[:, 0:1], extra[:, 1:2], extra[:, 2:3]], axis=2)
    rows_ref[...] = jnp.sum(whole[:, :, :384] * decoded_scale(step), axis=0)
    gains = (extra[:, 3:4] + extra[:, 4:5] * (1 / FULL)) * decoded_scale(extra[:, 5:6])
    gains_ref[...] = jnp.sum(gains, axis=0)[:, :8]


def shards(activations, norm_gain, qkv_weight, positions, cotangent):
    x_index = lax.axis_index("x")
    core = lax.axis_index("core")
    width = qkv_weight.shape[1]
    tokens = activations.shape[0]
    seed, own_weight = gather_plane(qkv_weight)
    normed = normalize(activations + jnp.tile(seed, (1, 8)), norm_gain)
    kept, received = redistribute(activations, x_index, core, seed)
    gain_part = lax.dynamic_slice(norm_gain.reshape(2, 8, 256), (0, x_index * 2 + core, 0), (2, 1, 256)).reshape(512)
    kept = prepared(kept, gain_part)
    received = prepared(received, gain_part)
    own_weight, normed, kept, received = lax.optimization_barrier((own_weight, normed, kept, received))
    positions = positions.reshape(tokens, 1)
    tables = rope_tables(positions, cotangent.shape[1], own_weight)

    place = jnp.stack([core, x_index * 2 + core])
    qkv_grads, weight_rows = attention_grads(place, own_weight, normed, tables, positions, cotangent)

    own_grads = lax.all_to_all(qkv_grads, "x", 0, 0, tiled=True)
    other_grads = swap_cores(own_grads)

    first = pl.pallas_call(
        first_grads_kernel,
        out_shape=(jax.ShapeDtypeStruct((512, width), jnp.float32), jax.ShapeDtypeStruct((512, 1), jnp.float32)),
        name="first_grads",
        compiler_params=pltpu.CompilerParams(vmem_limit_bytes=16 * 2**20),
        cost_estimate=BRIEF,
    )(*kept, own_grads, weight_rows)
    parts = pl.pallas_call(
        grads_kernel,
        out_shape=jax.ShapeDtypeStruct((8, 72, width), jnp.int16),
        scratch_shapes=[pltpu.VMEM((512, width), jnp.float32)],
        name="code_y",
        compiler_params=pltpu.CompilerParams(vmem_limit_bytes=16 * 2**20),
    )(*first, *received, other_grads, weight_rows)
    parts = lax.all_to_all(parts, ("y_hi", "y_lo", "core"), 0, 0, tiled=True)
    coded = pl.pallas_call(
        code_z_kernel, out_shape=jax.ShapeDtypeStruct((128, 512), jnp.int16), name="code_z", compiler_params=SMALL
    )(parts)
    coded = lax.all_to_all(coded, "z", 0, 0, tiled=True)
    share, gains = pl.pallas_call(
        decode_kernel,
        out_shape=(jax.ShapeDtypeStruct((8, width), jnp.float32), jax.ShapeDtypeStruct((1, 8), jnp.float32)),
        name="decode_rows", compiler_params=SMALL,
    )(coded)
    return share, gains.reshape(8)


def solution(mesh):
    fine = Mesh(mesh.devices.reshape(2, 4, 16, 2, 2), AXES)
    placed = (
        P(AXES, None),
        P(),
        P(("z", "y_lo", "core"), None),
        P(AXES),
        P(AXES, None),
    )
    return jax.shard_map(
        shards,
        mesh=fine,
        in_specs=placed,
        out_specs=(P(AXES, None), P(AXES)),
        check_vma=False,
    )
```

```python
import jax
import jax.numpy as jnp
from jax import lax
from jax.experimental import pallas as pl
from jax.experimental.pallas import tpu as pltpu
from jax.sharding import Mesh, PartitionSpec as P

rope_base = 10000.0
norm_eps = 1e-05


def angle_kernel(positions_ref, frequency_ref, after_ref, angles_ref):
    angles_ref[...] = positions_ref[...].astype(jnp.float32) * frequency_ref[...]


def rope_tables(positions, head_size, after):
    half_width = head_size // 2
    exponent = jnp.arange(half_width, dtype=jnp.float32) * (-2.0 / head_size)
    frequency = jnp.power(jnp.float32(rope_base), exponent)
    frequency = jnp.concatenate([frequency, frequency])[None]
    vmem = pl.BlockSpec(memory_space=pltpu.VMEM)
    angle_table = pl.pallas_call(
        angle_kernel,
        out_shape=jax.ShapeDtypeStruct((positions.shape[0], head_size), jnp.float32),
        in_specs=[vmem, vmem, pl.BlockSpec(memory_space=pl.ANY)],
        out_specs=vmem,
        name="angles",
        compiler_params=SMALL,
        cost_estimate=BRIEF,
    )(positions, frequency, after)
    return (jnp.cos(angle_table), jnp.sin(angle_table))


def normalize(activations, norm_gain):
    widened = activations.astype(jnp.float32)
    inverse_rms = lax.rsqrt(jnp.mean(widened * widened, axis=1, keepdims=True) + norm_eps)
    return (widened * inverse_rms * norm_gain[None, :]).astype(jnp.bfloat16)


def attention_kernel(
    core_ref, own_ref, other_ref, normed_ref, cosine_ref, sine_ref, positions_ref, cotangent_ref, grads_ref, rows_ref, weight_ref
):
    projected = project(core_ref, own_ref, other_ref, normed_ref, weight_ref, rows_ref)
    cosine, sine = cosine_ref[...], sine_ref[...]
    lower = lax.broadcasted_iota(jnp.int32, (128, 128), 1) < 64
    turned_sine = jnp.where(lower, -sine, sine)

    def rotate(part):
        return (part * cosine + pltpu.roll(part, 64, 1) * turned_sine).astype(jnp.bfloat16)

    def unrotate(part):
        return part * cosine + pltpu.roll(part * turned_sine, 64, 1)

    def product(left, right, over):
        return lax.dot_general(left, right, (((over[0],), (over[1],)), ((), ())), preferred_element_type=jnp.float32)

    queries, keys_rot = rotate(projected[:, :128]), rotate(projected[:, 128:256])
    values = projected[:, 256:].astype(jnp.bfloat16)
    cotangent = cotangent_ref[...]
    score_scale = 128 ** (-0.5)
    scores = product(queries, keys_rot, (1, 1)) * score_scale
    row_index = lax.broadcasted_iota(jnp.int32, (128, 128), 0)
    column_index = lax.broadcasted_iota(jnp.int32, (128, 128), 1)
    visible = (column_index <= row_index) & (row_index - column_index <= positions_ref[...])
    scores = jnp.where(visible, scores, -jnp.inf)
    exp_terms = jnp.exp(scores - jnp.max(scores, axis=1, keepdims=True))
    attention = exp_terms / jnp.sum(exp_terms, axis=1, keepdims=True)
    attention_low = attention.astype(jnp.bfloat16)
    prob_grad = product(cotangent, values, (1, 1))
    score_grad = (
        attention * (prob_grad - jnp.sum(attention * prob_grad, axis=1, keepdims=True)) * score_scale
    ).astype(jnp.bfloat16)
    grads = jnp.concatenate(
        [
            unrotate(product(score_grad, keys_rot, (1, 0))),
            unrotate(product(score_grad, queries, (0, 0))),
            product(attention_low, cotangent, (0, 0)),
        ],
        axis=1,
    ).astype(jnp.bfloat16)
    for copy in range(4):
        grads_ref[copy] = grads


def attention_grads(place, own, normed, tables, positions, cotangent):
    tokens, width = normed.shape[0], own.shape[1]
    raw = own.reshape(8, 2, 16, 8, width)
    ordered = pl.pallas_call(
        order_kernel,
        out_shape=jax.ShapeDtypeStruct((16, 2, 64, width), own.dtype),
        name="order_rows",
        compiler_params=SMALL,
        cost_estimate=BRIEF,
    )(raw)
    vmem = pl.BlockSpec(memory_space=pltpu.VMEM)
    grads, rows = pl.pallas_call(
        attention_kernel,
        out_shape=(
            jax.ShapeDtypeStruct((4, tokens, width), jnp.bfloat16),
            jax.ShapeDtypeStruct((512, width), jnp.bfloat16),
        ),
        in_specs=[pl.BlockSpec(memory_space=pltpu.SMEM)] + [vmem] * 7,
        out_specs=(vmem, vmem),
        scratch_shapes=[pltpu.VMEM((4096, width), jnp.bfloat16)],
        name="attention_grads",
        compiler_params=pltpu.CompilerParams(vmem_limit_bytes=20 * 2**20),
    )(place, ordered, swap_cores(own).reshape(raw.shape), normed, *tables, positions, cotangent)
    return grads.reshape(4 * tokens, width), rows


AXES = ("y_hi", "x", "z", "y_lo", "core")
Z_ORDER = [[(place + 8) % 16 for place in range(16)]]
STEPS = 64.0
BRIEF = pl.CostEstimate(flops=2**20, bytes_accessed=2**18, transcendentals=0)
SMALL = pltpu.CompilerParams(vmem_limit_bytes=8 * 2**20)
FULL = 32767.0


def broadcast_rows(block, count):
    rows, width = block.shape
    return jnp.broadcast_to(block[None], (count, rows, width)).reshape(count * rows, width)


def swap_cores(array):
    return lax.ppermute(array, "core", [(0, 1), (1, 0)])


def copy_kernel(part_ref, copies_ref, seed_ref):
    for copy in range(16):
        copies_ref[copy, pl.ds(0, 64), :] = part_ref[pl.ds(64, 64), :]
        copies_ref[copy, pl.ds(64, 64), :] = part_ref[pl.ds(0, 64), :]
    seed_ref[...] = jnp.zeros_like(seed_ref)


def gather_plane(qkv_weight):
    width = qkv_weight.shape[1]
    member = lax.axis_index("y_hi") * 4 + lax.axis_index("x")
    part = lax.dynamic_slice(qkv_weight, (member * 8, 0), (8, width))
    along_z = lax.all_to_all(broadcast_rows(part, 16), "z", 0, 0, axis_index_groups=Z_ORDER, tiled=True)
    copies, seed = pl.pallas_call(
        copy_kernel,
        out_shape=(jax.ShapeDtypeStruct((16, 128, width), jnp.bfloat16), jax.ShapeDtypeStruct((1, 512), jnp.bfloat16)),
        name="copy_rows",
        compiler_params=SMALL,
    )(along_z)
    plane = lax.all_to_all(copies.reshape(2048, width), ("y_hi", "x", "y_lo"), 0, 0, tiled=True)
    return seed, plane


def order_kernel(raw_ref, ordered_ref):
    for z in range(16):
        for y in range(2):
            rows = [raw_ref[eighth, y, z].astype(jnp.float32) for eighth in range(8)]
            ordered_ref[z, y] = jnp.concatenate(rows).astype(jnp.bfloat16)


def project(core_ref, own_ref, other_ref, normed_ref, weight_ref, rows_ref):
    core, column = core_ref[0], core_ref[1]
    for z in range(16):
        for y in range(2):
            rows = [other_ref[eighth, y, z].astype(jnp.float32) for eighth in range(8)]
            place = z * 256 + y * 128
            weight_ref[pl.ds(pl.multiple_of(place + core * 64, 64), 64), :] = own_ref[z, y]
            weight_ref[pl.ds(pl.multiple_of(place + (1 - core) * 64, 64), 64), :] = jnp.concatenate(rows).astype(jnp.bfloat16)
    for half in range(2):
        start = pl.multiple_of(half * 2048 + column * 256, 256)
        rows_ref[pl.ds(half * 256, 256), :] = weight_ref[pl.ds(start, 256), :]
    return jnp.dot(normed_ref[...], weight_ref[...], preferred_element_type=jnp.float32)


def blocks_kernel(x_ref, activations_ref, *block_refs):
    squares = 0.0
    for part in range(4):
        widened = activations_ref[:, part * 1024 : (part + 1) * 1024].astype(jnp.float32)
        squares += jnp.sum(widened * widened, axis=1, keepdims=True)
    inverse_rms = jnp.broadcast_to(lax.rsqrt(squares / 4096 + norm_eps), (128, 128)).T
    high = inverse_rms.astype(jnp.bfloat16).astype(jnp.float32)
    rest = inverse_rms - high
    middle = rest.astype(jnp.bfloat16).astype(jnp.float32)
    row = lax.broadcasted_iota(jnp.int32, (128, 128), 0)
    extra = jnp.where(row == 0, high, jnp.where(row == 1, middle, jnp.where(row == 2, rest - middle, 0.0)))
    extra = jnp.concatenate([extra[:16]] * 4, axis=1).astype(jnp.bfloat16)
    for shift, block_ref in enumerate(block_refs):
        target = lax.rem(x_ref[0] + shift, 4)
        for half in range(2):
            start = pl.multiple_of(half * 2048 + target * 512, 512)
            block_ref[half, pl.ds(0, 128), :] = activations_ref[:, pl.ds(start, 512)]
            block_ref[half, pl.ds(128, 16), :] = extra


def redistribute(activations, x_index, core, seed):
    tokens = activations.shape[0]
    vmem = pl.BlockSpec(memory_space=pltpu.VMEM)
    blocks = pl.pallas_call(
        blocks_kernel,
        out_shape=[jax.ShapeDtypeStruct((2, tokens + 16, 512), jnp.bfloat16)] * 4,
        in_specs=[pl.BlockSpec(memory_space=pltpu.SMEM), vmem],
        out_specs=[vmem] * 4,
        name="cut_blocks",
        compiler_params=SMALL,
        cost_estimate=BRIEF,
    )(x_index.reshape(1), activations)
    ordered = jnp.broadcast_to(seed.reshape(1, 1, 1, 512), (4, 2, tokens + 16, 512))
    for shift, block in enumerate(blocks):
        if shift:
            block = lax.ppermute(block, "x", [(i, (i + shift) % 4) for i in range(4)])
        ordered = lax.dynamic_update_slice(ordered, block[None], (lax.rem(x_index - shift + 4, 4), 0, 0, 0))
    first, second = ordered[..., :256], ordered[..., 256:]
    kept = jnp.where(core == 0, first, second)
    sent = jnp.where(core == 0, second, first)
    return kept, swap_cores(sent)


def prepare_kernel(block_ref, gain_ref, normed_ref, unit_ref):
    for x in range(4):
        for half in range(2):
            block = block_ref[x, half].astype(jnp.float32)
            inverse_rms = (block[128:129, :128] + block[129:130, :128]) + block[130:131, :128]
            unit = block[:128].T * inverse_rms
            place = (pl.ds(half * 256, 256), pl.ds(x * 128, 128))
            unit_ref[place] = unit
            normed_ref[place] = (unit * gain_ref[pl.ds(half * 256, 256), :]).astype(jnp.bfloat16)


def prepared(block, gain_part):
    return pl.pallas_call(
        prepare_kernel,
        out_shape=(jax.ShapeDtypeStruct((512, 512), jnp.bfloat16), jax.ShapeDtypeStruct((512, 512), jnp.float32)),
        name="prepare_columns",
        compiler_params=pltpu.CompilerParams(vmem_limit_bytes=16 * 2**20),
    )(block, gain_part.reshape(512, 1))


def step_of(values, axis):
    peak = jnp.max(jnp.abs(values), axis=axis, keepdims=True)
    return jnp.clip(jnp.ceil(jnp.log2(peak) * STEPS), -110 * STEPS, 127 * STEPS)


def coded_values(values, step):
    return jnp.clip(jnp.round(values * (jnp.exp2(step * (-1 / STEPS)) * FULL)), -FULL, FULL)


def decoded_scale(step):
    return jnp.exp2(step * (1 / STEPS)) * (1 / FULL)


def coded_gain(gains):
    step = step_of(gains, -1)
    exact = gains * (jnp.exp2(step * (-1 / STEPS)) * FULL)
    high = jnp.clip(jnp.round(exact), -FULL, FULL)
    low = jnp.clip(jnp.round((exact - high) * FULL), -FULL, FULL)
    return high, low, jnp.broadcast_to(step, gains.shape)


def narrow(values):
    return values.astype(jnp.int32).astype(jnp.int16)


def wide(codes):
    return codes.astype(jnp.int32).astype(jnp.float32)


def half_grads(normed_ref, unit_ref, grads_ref, rows_ref):
    term = jnp.dot(normed_ref[...], grads_ref[...], preferred_element_type=jnp.float32)
    normed_grad = lax.dot_general(
        rows_ref[...], grads_ref[...], (((1,), (1,)), ((), ())), preferred_element_type=jnp.float32
    )
    return term, jnp.sum(normed_grad * unit_ref[...], axis=1, keepdims=True)


def first_grads_kernel(normed_ref, unit_ref, grads_ref, rows_ref, term_ref, gain_ref):
    term_ref[...], gain_ref[...] = half_grads(normed_ref, unit_ref, grads_ref, rows_ref)


def grads_kernel(first_ref, first_gain_ref, normed_ref, unit_ref, grads_ref, rows_ref, coded_ref, term_ref):
    term, gain = half_grads(normed_ref, unit_ref, grads_ref, rows_ref)
    term_ref[...] = first_ref[...] + term
    gain = first_gain_ref[...] + gain
    lanes = lax.broadcasted_iota(jnp.int32, (64, 128), 1)
    table = jnp.zeros((64, 128), jnp.float32)
    for chunk in range(8):
        first = chunk // 4 * 256 + chunk % 4 * 8
        column = jnp.concatenate([gain[first + z * 32 : first + z * 32 + 8] for z in range(8)])
        table = jnp.where(lanes == chunk, column, table)
    table = jnp.concatenate([table, jnp.zeros((64, 128), jnp.float32)]).T
    gains = coded_gain(table[:8])
    for chunk in range(8):
        first = chunk // 4 * 256 + chunk % 4 * 8
        rows = jnp.concatenate([term_ref[pl.ds(first + z * 32, 8), :] for z in range(8)])
        step = step_of(rows, 0)
        shown = [jnp.pad(part[chunk : chunk + 1], ((0, 0), (0, 256))) for part in gains]
        whole = [coded_values(rows, step), step] + shown + [jnp.zeros((4, 384), jnp.float32)]
        coded_ref[chunk] = narrow(jnp.concatenate(whole))


def code_z_kernel(parts_ref, coded_ref):
    rows, gains = [], []
    for core in range(2):
        row_sum, gain_sum = 0.0, 0.0
        for y in range(4):
            part = wide(parts_ref[y * 2 + core])
            extra = part[64:]
            row_sum += part[:64] * decoded_scale(extra[0:1])
            gain_sum += (extra[1:2, :128] + extra[2:3, :128] * (1 / FULL)) * decoded_scale(extra[3:4, :128])
        rows.append(row_sum)
        gains.append(gain_sum)
    rows = jnp.concatenate(rows).reshape(16, 8, 384)
    step = step_of(rows, 1)
    shown = jnp.concatenate(coded_gain(jnp.concatenate(gains)) + (jnp.zeros((2, 128), jnp.float32),))
    extra = []
    for z in range(16):
        moved = shown if z % 8 == 0 else pltpu.roll(shown, 128 - z % 8 * 8, 1)
        core = z // 8
        extra.append(jnp.concatenate(
            [step[z, :, k * 128 : (k + 1) * 128] for k in range(3)]
            + [moved[k + core : k + core + 1] for k in (0, 2, 4)]
            + [jnp.zeros((2, 128), jnp.float32)]
        ))
    whole = jnp.concatenate([coded_values(rows, step).reshape(128, 384), jnp.concatenate(extra)], axis=1)
    coded_ref[...] = narrow(jnp.concatenate([whole[64:], whole[:64]]))


def decode_kernel(coded_ref, rows_ref, gains_ref):
    whole = wide(coded_ref[...]).reshape(16, 8, 512)
    extra = whole[:, :, 384:]
    step = jnp.concatenate([extra[:, 0:1], extra[:, 1:2], extra[:, 2:3]], axis=2)
    rows_ref[...] = jnp.sum(whole[:, :, :384] * decoded_scale(step), axis=0)
    gains = (extra[:, 3:4] + extra[:, 4:5] * (1 / FULL)) * decoded_scale(extra[:, 5:6])
    gains_ref[...] = jnp.sum(gains, axis=0)[:, :8]


def shards(activations, norm_gain, qkv_weight, positions, cotangent):
    x_index = lax.axis_index("x")
    core = lax.axis_index("core")
    width = qkv_weight.shape[1]
    tokens = activations.shape[0]
    seed, own_weight = gather_plane(qkv_weight)
    normed = normalize(activations + jnp.tile(seed, (1, 8)), norm_gain)
    kept, received = redistribute(activations, x_index, core, seed)
    gain_part = lax.dynamic_slice(norm_gain.reshape(2, 8, 256), (0, x_index * 2 + core, 0), (2, 1, 256)).reshape(512)
    kept = prepared(kept, gain_part)
    received = prepared(received, gain_part)
    own_weight, normed, kept, received = lax.optimization_barrier((own_weight, normed, kept, received))
    positions = positions.reshape(tokens, 1)
    tables = rope_tables(positions, cotangent.shape[1], own_weight)

    place = jnp.stack([core, x_index * 2 + core])
    qkv_grads, weight_rows = attention_grads(place, own_weight, normed, tables, positions, cotangent)

    own_grads = lax.all_to_all(qkv_grads, "x", 0, 0, tiled=True)
    other_grads = swap_cores(own_grads)

    first = pl.pallas_call(
        first_grads_kernel,
        out_shape=(jax.ShapeDtypeStruct((512, width), jnp.float32), jax.ShapeDtypeStruct((512, 1), jnp.float32)),
        name="first_grads",
        compiler_params=pltpu.CompilerParams(vmem_limit_bytes=16 * 2**20),
        cost_estimate=BRIEF,
    )(*kept, own_grads, weight_rows)
    parts = pl.pallas_call(
        grads_kernel,
        out_shape=jax.ShapeDtypeStruct((8, 72, width), jnp.int16),
        scratch_shapes=[pltpu.VMEM((512, width), jnp.float32)],
        name="code_y",
        compiler_params=pltpu.CompilerParams(vmem_limit_bytes=16 * 2**20),
    )(*first, *received, other_grads, weight_rows)
    parts = lax.all_to_all(parts, ("y_hi", "y_lo", "core"), 0, 0, tiled=True)
    coded = pl.pallas_call(
        code_z_kernel, out_shape=jax.ShapeDtypeStruct((128, 512), jnp.int16), name="code_z", compiler_params=SMALL
    )(parts)
    coded = lax.all_to_all(coded, "z", 0, 0, axis_index_groups=Z_ORDER, tiled=True)
    share, gains = pl.pallas_call(
        decode_kernel,
        out_shape=(jax.ShapeDtypeStruct((8, width), jnp.float32), jax.ShapeDtypeStruct((1, 8), jnp.float32)),
        name="decode_rows", compiler_params=SMALL,
    )(coded)
    return share, gains.reshape(8)


def solution(mesh):
    fine = Mesh(mesh.devices.reshape(2, 4, 16, 2, 2), AXES)
    placed = (
        P(AXES, None),
        P(),
        P(("z", "y_lo", "core"), None),
        P(AXES),
        P(AXES, None),
    )
    return jax.shard_map(
        shards,
        mesh=fine,
        in_specs=placed,
        out_specs=(P(AXES, None), P(AXES)),
        check_vma=False,
    )
```

```python
import jax
import jax.numpy as jnp
from jax import lax
from jax.experimental import pallas as pl
from jax.experimental.pallas import tpu as pltpu
from jax.sharding import Mesh, PartitionSpec as P

rope_base = 10000.0
norm_eps = 1e-05


def angle_kernel(positions_ref, frequency_ref, after_ref, angles_ref):
    angles_ref[...] = positions_ref[...].astype(jnp.float32) * frequency_ref[...]


def rope_tables(positions, head_size, after):
    half_width = head_size // 2
    exponent = jnp.arange(half_width, dtype=jnp.float32) * (-2.0 / head_size)
    frequency = jnp.power(jnp.float32(rope_base), exponent)
    frequency = jnp.concatenate([frequency, frequency])[None]
    vmem = pl.BlockSpec(memory_space=pltpu.VMEM)
    angle_table = pl.pallas_call(
        angle_kernel,
        out_shape=jax.ShapeDtypeStruct((positions.shape[0], head_size), jnp.float32),
        in_specs=[vmem, vmem, pl.BlockSpec(memory_space=pl.ANY)],
        out_specs=vmem,
        name="angles",
        compiler_params=SMALL,
        cost_estimate=BRIEF,
    )(positions, frequency, after)
    return (jnp.cos(angle_table), jnp.sin(angle_table))


def normalize(activations, norm_gain):
    widened = activations.astype(jnp.float32)
    inverse_rms = lax.rsqrt(jnp.mean(widened * widened, axis=1, keepdims=True) + norm_eps)
    return (widened * inverse_rms * norm_gain[None, :]).astype(jnp.bfloat16)


def attention_kernel(
    core_ref, own_ref, other_ref, normed_ref, cosine_ref, sine_ref, positions_ref, cotangent_ref, grads_ref, rows_ref, weight_ref
):
    projected = project(core_ref, own_ref, other_ref, normed_ref, weight_ref, rows_ref)
    cosine, sine = cosine_ref[...], sine_ref[...]
    lower = lax.broadcasted_iota(jnp.int32, (128, 128), 1) < 64
    turned_sine = jnp.where(lower, -sine, sine)

    def rotate(part):
        return (part * cosine + pltpu.roll(part, 64, 1) * turned_sine).astype(jnp.bfloat16)

    def unrotate(part):
        return part * cosine + pltpu.roll(part * turned_sine, 64, 1)

    def product(left, right, over):
        return lax.dot_general(left, right, (((over[0],), (over[1],)), ((), ())), preferred_element_type=jnp.float32)

    queries, keys_rot = rotate(projected[:, :128]), rotate(projected[:, 128:256])
    values = projected[:, 256:].astype(jnp.bfloat16)
    cotangent = cotangent_ref[...]
    score_scale = 128 ** (-0.5)
    scores = product(queries, keys_rot, (1, 1)) * score_scale
    row_index = lax.broadcasted_iota(jnp.int32, (128, 128), 0)
    column_index = lax.broadcasted_iota(jnp.int32, (128, 128), 1)
    visible = (column_index <= row_index) & (row_index - column_index <= positions_ref[...])
    scores = jnp.where(visible, scores, -jnp.inf)
    exp_terms = jnp.exp(scores - jnp.max(scores, axis=1, keepdims=True))
    attention = exp_terms / jnp.sum(exp_terms, axis=1, keepdims=True)
    attention_low = attention.astype(jnp.bfloat16)
    prob_grad = product(cotangent, values, (1, 1))
    score_grad = (
        attention * (prob_grad - jnp.sum(attention * prob_grad, axis=1, keepdims=True)) * score_scale
    ).astype(jnp.bfloat16)
    grads = jnp.concatenate(
        [
            unrotate(product(score_grad, keys_rot, (1, 0))),
            unrotate(product(score_grad, queries, (0, 0))),
            product(attention_low, cotangent, (0, 0)),
        ],
        axis=1,
    ).astype(jnp.bfloat16)
    for copy in range(4):
        grads_ref[copy] = grads


def attention_grads(place, own, normed, tables, positions, cotangent):
    tokens, width = normed.shape[0], own.shape[1]
    raw = own.reshape(8, 2, 16, 8, width)
    ordered = pl.pallas_call(
        order_kernel,
        out_shape=jax.ShapeDtypeStruct((16, 2, 64, width), own.dtype),
        name="order_rows",
        compiler_params=SMALL,
        cost_estimate=BRIEF,
    )(raw)
    vmem = pl.BlockSpec(memory_space=pltpu.VMEM)
    grads, rows = pl.pallas_call(
        attention_kernel,
        out_shape=(
            jax.ShapeDtypeStruct((4, tokens, width), jnp.bfloat16),
            jax.ShapeDtypeStruct((512, width), jnp.bfloat16),
        ),
        in_specs=[pl.BlockSpec(memory_space=pltpu.SMEM)] + [vmem] * 7,
        out_specs=(vmem, vmem),
        scratch_shapes=[pltpu.VMEM((4096, width), jnp.bfloat16)],
        name="attention_grads",
        compiler_params=pltpu.CompilerParams(vmem_limit_bytes=20 * 2**20),
    )(place, ordered, swap_cores(own).reshape(raw.shape), normed, *tables, positions, cotangent)
    return grads.reshape(4 * tokens, width), rows


AXES = ("y_hi", "x", "z", "y_lo", "core")
FIRST_Z, LAST_Z = 12, 4
FIRST_ORDER, LAST_ORDER = ([[(place + start) % 16 for place in range(16)]] for start in (FIRST_Z, LAST_Z))
STEPS = 64.0
BRIEF = pl.CostEstimate(flops=2**20, bytes_accessed=2**18, transcendentals=0)
SMALL = pltpu.CompilerParams(vmem_limit_bytes=8 * 2**20)
FULL = 32767.0


def broadcast_rows(block, count):
    rows, width = block.shape
    return jnp.broadcast_to(block[None], (count, rows, width)).reshape(count * rows, width)


def swap_cores(array):
    return lax.ppermute(array, "core", [(0, 1), (1, 0)])


def copy_kernel(part_ref, copies_ref, seed_ref):
    late = FIRST_Z * 8
    for copy in range(16):
        copies_ref[copy, pl.ds(0, late), :] = part_ref[pl.ds(128 - late, late), :]
        copies_ref[copy, pl.ds(late, 128 - late), :] = part_ref[pl.ds(0, 128 - late), :]
    seed_ref[...] = jnp.zeros_like(seed_ref)


def gather_plane(qkv_weight):
    width = qkv_weight.shape[1]
    member = lax.axis_index("y_hi") * 4 + lax.axis_index("x")
    part = lax.dynamic_slice(qkv_weight, (member * 8, 0), (8, width))
    along_z = lax.all_to_all(broadcast_rows(part, 16), "z", 0, 0, axis_index_groups=FIRST_ORDER, tiled=True)
    copies, seed = pl.pallas_call(
        copy_kernel,
        out_shape=(jax.ShapeDtypeStruct((16, 128, width), jnp.bfloat16), jax.ShapeDtypeStruct((1, 512), jnp.bfloat16)),
        name="copy_rows",
        compiler_params=SMALL,
    )(along_z)
    plane = lax.all_to_all(copies.reshape(2048, width), ("y_hi", "x", "y_lo"), 0, 0, tiled=True)
    return seed, plane


def order_kernel(raw_ref, ordered_ref):
    for z in range(16):
        for y in range(2):
            rows = [raw_ref[eighth, y, z].astype(jnp.float32) for eighth in range(8)]
            ordered_ref[z, y] = jnp.concatenate(rows).astype(jnp.bfloat16)


def project(core_ref, own_ref, other_ref, normed_ref, weight_ref, rows_ref):
    core, column = core_ref[0], core_ref[1]
    for z in range(16):
        for y in range(2):
            rows = [other_ref[eighth, y, z].astype(jnp.float32) for eighth in range(8)]
            place = z * 256 + y * 128
            weight_ref[pl.ds(pl.multiple_of(place + core * 64, 64), 64), :] = own_ref[z, y]
            weight_ref[pl.ds(pl.multiple_of(place + (1 - core) * 64, 64), 64), :] = jnp.concatenate(rows).astype(jnp.bfloat16)
    for half in range(2):
        start = pl.multiple_of(half * 2048 + column * 256, 256)
        rows_ref[pl.ds(half * 256, 256), :] = weight_ref[pl.ds(start, 256), :]
    return jnp.dot(normed_ref[...], weight_ref[...], preferred_element_type=jnp.float32)


def blocks_kernel(x_ref, activations_ref, *block_refs):
    squares = 0.0
    for part in range(4):
        widened = activations_ref[:, part * 1024 : (part + 1) * 1024].astype(jnp.float32)
        squares += jnp.sum(widened * widened, axis=1, keepdims=True)
    inverse_rms = jnp.broadcast_to(lax.rsqrt(squares / 4096 + norm_eps), (128, 128)).T
    high = inverse_rms.astype(jnp.bfloat16).astype(jnp.float32)
    rest = inverse_rms - high
    middle = rest.astype(jnp.bfloat16).astype(jnp.float32)
    row = lax.broadcasted_iota(jnp.int32, (128, 128), 0)
    extra = jnp.where(row == 0, high, jnp.where(row == 1, middle, jnp.where(row == 2, rest - middle, 0.0)))
    extra = jnp.concatenate([extra[:16]] * 4, axis=1).astype(jnp.bfloat16)
    for shift, block_ref in enumerate(block_refs):
        target = lax.rem(x_ref[0] + shift, 4)
        for half in range(2):
            start = pl.multiple_of(half * 2048 + target * 512, 512)
            block_ref[half, pl.ds(0, 128), :] = activations_ref[:, pl.ds(start, 512)]
            block_ref[half, pl.ds(128, 16), :] = extra


def redistribute(activations, x_index, core, seed):
    tokens = activations.shape[0]
    vmem = pl.BlockSpec(memory_space=pltpu.VMEM)
    blocks = pl.pallas_call(
        blocks_kernel,
        out_shape=[jax.ShapeDtypeStruct((2, tokens + 16, 512), jnp.bfloat16)] * 4,
        in_specs=[pl.BlockSpec(memory_space=pltpu.SMEM), vmem],
        out_specs=[vmem] * 4,
        name="cut_blocks",
        compiler_params=SMALL,
        cost_estimate=BRIEF,
    )(x_index.reshape(1), activations)
    ordered = jnp.broadcast_to(seed.reshape(1, 1, 1, 512), (4, 2, tokens + 16, 512))
    for shift, block in enumerate(blocks):
        if shift:
            block = lax.ppermute(block, "x", [(i, (i + shift) % 4) for i in range(4)])
        ordered = lax.dynamic_update_slice(ordered, block[None], (lax.rem(x_index - shift + 4, 4), 0, 0, 0))
    first, second = ordered[..., :256], ordered[..., 256:]
    kept = jnp.where(core == 0, first, second)
    sent = jnp.where(core == 0, second, first)
    return kept, swap_cores(sent)


def prepare_kernel(block_ref, gain_ref, normed_ref, unit_ref):
    for x in range(4):
        for half in range(2):
            block = block_ref[x, half].astype(jnp.float32)
            inverse_rms = (block[128:129, :128] + block[129:130, :128]) + block[130:131, :128]
            unit = block[:128].T * inverse_rms
            place = (pl.ds(half * 256, 256), pl.ds(x * 128, 128))
            unit_ref[place] = unit
            normed_ref[place] = (unit * gain_ref[pl.ds(half * 256, 256), :]).astype(jnp.bfloat16)


def prepared(block, gain_part):
    return pl.pallas_call(
        prepare_kernel,
        out_shape=(jax.ShapeDtypeStruct((512, 512), jnp.bfloat16), jax.ShapeDtypeStruct((512, 512), jnp.float32)),
        name="prepare_columns",
        compiler_params=pltpu.CompilerParams(vmem_limit_bytes=16 * 2**20),
    )(block, gain_part.reshape(512, 1))


def step_of(values, axis):
    peak = jnp.max(jnp.abs(values), axis=axis, keepdims=True)
    return jnp.clip(jnp.ceil(jnp.log2(peak) * STEPS), -110 * STEPS, 127 * STEPS)


def coded_values(values, step):
    return jnp.clip(jnp.round(values * (jnp.exp2(step * (-1 / STEPS)) * FULL)), -FULL, FULL)


def decoded_scale(step):
    return jnp.exp2(step * (1 / STEPS)) * (1 / FULL)


def coded_gain(gains):
    step = step_of(gains, -1)
    exact = gains * (jnp.exp2(step * (-1 / STEPS)) * FULL)
    high = jnp.clip(jnp.round(exact), -FULL, FULL)
    low = jnp.clip(jnp.round((exact - high) * FULL), -FULL, FULL)
    return high, low, jnp.broadcast_to(step, gains.shape)


def narrow(values):
    return values.astype(jnp.int32).astype(jnp.int16)


def wide(codes):
    return codes.astype(jnp.int32).astype(jnp.float32)


def half_grads(normed_ref, unit_ref, grads_ref, rows_ref):
    term = jnp.dot(normed_ref[...], grads_ref[...], preferred_element_type=jnp.float32)
    normed_grad = lax.dot_general(
        rows_ref[...], grads_ref[...], (((1,), (1,)), ((), ())), preferred_element_type=jnp.float32
    )
    return term, jnp.sum(normed_grad * unit_ref[...], axis=1, keepdims=True)


def first_grads_kernel(normed_ref, unit_ref, grads_ref, rows_ref, term_ref, gain_ref):
    term_ref[...], gain_ref[...] = half_grads(normed_ref, unit_ref, grads_ref, rows_ref)


def grads_kernel(first_ref, first_gain_ref, normed_ref, unit_ref, grads_ref, rows_ref, coded_ref, term_ref):
    term, gain = half_grads(normed_ref, unit_ref, grads_ref, rows_ref)
    term_ref[...] = first_ref[...] + term
    gain = first_gain_ref[...] + gain
    lanes = lax.broadcasted_iota(jnp.int32, (64, 128), 1)
    table = jnp.zeros((64, 128), jnp.float32)
    for chunk in range(8):
        first = chunk // 4 * 256 + chunk % 4 * 8
        column = jnp.concatenate([gain[first + z * 32 : first + z * 32 + 8] for z in range(8)])
        table = jnp.where(lanes == chunk, column, table)
    table = jnp.concatenate([table, jnp.zeros((64, 128), jnp.float32)]).T
    gains = coded_gain(table[:8])
    for chunk in range(8):
        first = chunk // 4 * 256 + chunk % 4 * 8
        rows = jnp.concatenate([term_ref[pl.ds(first + z * 32, 8), :] for z in range(8)])
        step = step_of(rows, 0)
        shown = [jnp.pad(part[chunk : chunk + 1], ((0, 0), (0, 256))) for part in gains]
        whole = [coded_values(rows, step), step] + shown + [jnp.zeros((4, 384), jnp.float32)]
        coded_ref[chunk] = narrow(jnp.concatenate(whole))


def code_z_kernel(parts_ref, coded_ref):
    rows, gains = [], []
    for core in range(2):
        row_sum, gain_sum = 0.0, 0.0
        for y in range(4):
            part = wide(parts_ref[y * 2 + core])
            extra = part[64:]
            row_sum += part[:64] * decoded_scale(extra[0:1])
            gain_sum += (extra[1:2, :128] + extra[2:3, :128] * (1 / FULL)) * decoded_scale(extra[3:4, :128])
        rows.append(row_sum)
        gains.append(gain_sum)
    rows = jnp.concatenate(rows).reshape(16, 8, 384)
    step = step_of(rows, 1)
    shown = jnp.concatenate(coded_gain(jnp.concatenate(gains)) + (jnp.zeros((2, 128), jnp.float32),))
    extra = []
    for z in range(16):
        moved = shown if z % 8 == 0 else pltpu.roll(shown, 128 - z % 8 * 8, 1)
        core = z // 8
        extra.append(jnp.concatenate(
            [step[z, :, k * 128 : (k + 1) * 128] for k in range(3)]
            + [moved[k + core : k + core + 1] for k in (0, 2, 4)]
            + [jnp.zeros((2, 128), jnp.float32)]
        ))
    whole = jnp.concatenate([coded_values(rows, step).reshape(128, 384), jnp.concatenate(extra)], axis=1)
    coded_ref[...] = narrow(jnp.concatenate([whole[LAST_Z * 8 :], whole[: LAST_Z * 8]]))


def decode_kernel(coded_ref, rows_ref, gains_ref):
    whole = wide(coded_ref[...]).reshape(16, 8, 512)
    extra = whole[:, :, 384:]
    step = jnp.concatenate([extra[:, 0:1], extra[:, 1:2], extra[:, 2:3]], axis=2)
    rows_ref[...] = jnp.sum(whole[:, :, :384] * decoded_scale(step), axis=0)
    gains = (extra[:, 3:4] + extra[:, 4:5] * (1 / FULL)) * decoded_scale(extra[:, 5:6])
    gains_ref[...] = jnp.sum(gains, axis=0)[:, :8]


def shards(activations, norm_gain, qkv_weight, positions, cotangent):
    x_index = lax.axis_index("x")
    core = lax.axis_index("core")
    width = qkv_weight.shape[1]
    tokens = activations.shape[0]
    seed, own_weight = gather_plane(qkv_weight)
    normed = normalize(activations + jnp.tile(seed, (1, 8)), norm_gain)
    kept, received = redistribute(activations, x_index, core, seed)
    gain_part = lax.dynamic_slice(norm_gain.reshape(2, 8, 256), (0, x_index * 2 + core, 0), (2, 1, 256)).reshape(512)
    kept = prepared(kept, gain_part)
    received = prepared(received, gain_part)
    own_weight, normed, kept, received = lax.optimization_barrier((own_weight, normed, kept, received))
    positions = positions.reshape(tokens, 1)
    tables = rope_tables(positions, cotangent.shape[1], own_weight)

    place = jnp.stack([core, x_index * 2 + core])
    qkv_grads, weight_rows = attention_grads(place, own_weight, normed, tables, positions, cotangent)

    own_grads = lax.all_to_all(qkv_grads, "x", 0, 0, tiled=True)
    other_grads = swap_cores(own_grads)

    first = pl.pallas_call(
        first_grads_kernel,
        out_shape=(jax.ShapeDtypeStruct((512, width), jnp.float32), jax.ShapeDtypeStruct((512, 1), jnp.float32)),
        name="first_grads",
        compiler_params=pltpu.CompilerParams(vmem_limit_bytes=16 * 2**20),
        cost_estimate=BRIEF,
    )(*kept, own_grads, weight_rows)
    parts = pl.pallas_call(
        grads_kernel,
        out_shape=jax.ShapeDtypeStruct((8, 72, width), jnp.int16),
        scratch_shapes=[pltpu.VMEM((512, width), jnp.float32)],
        name="code_y",
        compiler_params=pltpu.CompilerParams(vmem_limit_bytes=16 * 2**20),
    )(*first, *received, other_grads, weight_rows)
    parts = lax.all_to_all(parts, ("y_hi", "y_lo", "core"), 0, 0, tiled=True)
    coded = pl.pallas_call(
        code_z_kernel, out_shape=jax.ShapeDtypeStruct((128, 512), jnp.int16), name="code_z", compiler_params=SMALL
    )(parts)
    coded = lax.all_to_all(coded, "z", 0, 0, axis_index_groups=LAST_ORDER, tiled=True)
    share, gains = pl.pallas_call(
        decode_kernel,
        out_shape=(jax.ShapeDtypeStruct((8, width), jnp.float32), jax.ShapeDtypeStruct((1, 8), jnp.float32)),
        name="decode_rows", compiler_params=SMALL,
    )(coded)
    return share, gains.reshape(8)


def solution(mesh):
    fine = Mesh(mesh.devices.reshape(2, 4, 16, 2, 2), AXES)
    placed = (
        P(AXES, None),
        P(),
        P(("z", "y_lo", "core"), None),
        P(AXES),
        P(AXES, None),
    )
    return jax.shard_map(
        shards,
        mesh=fine,
        in_specs=placed,
        out_specs=(P(AXES, None), P(AXES)),
        check_vma=False,
    )
```

```python
import jax
import jax.numpy as jnp
from jax import lax
from jax.experimental import pallas as pl
from jax.experimental.pallas import tpu as pltpu
from jax.sharding import Mesh, PartitionSpec as P

rope_base = 10000.0
norm_eps = 1e-05


def angle_kernel(positions_ref, frequency_ref, after_ref, angles_ref):
    angles_ref[...] = positions_ref[...].astype(jnp.float32) * frequency_ref[...]


def rope_tables(positions, head_size, after):
    half_width = head_size // 2
    exponent = jnp.arange(half_width, dtype=jnp.float32) * (-2.0 / head_size)
    frequency = jnp.power(jnp.float32(rope_base), exponent)
    frequency = jnp.concatenate([frequency, frequency])[None]
    vmem = pl.BlockSpec(memory_space=pltpu.VMEM)
    angle_table = pl.pallas_call(
        angle_kernel,
        out_shape=jax.ShapeDtypeStruct((positions.shape[0], head_size), jnp.float32),
        in_specs=[vmem, vmem, pl.BlockSpec(memory_space=pl.ANY)],
        out_specs=vmem,
        name="angles",
        compiler_params=SMALL,
        cost_estimate=BRIEF,
    )(positions, frequency, after)
    return (jnp.cos(angle_table), jnp.sin(angle_table))


def normalize(activations, norm_gain):
    widened = activations.astype(jnp.float32)
    inverse_rms = lax.rsqrt(jnp.mean(widened * widened, axis=1, keepdims=True) + norm_eps)
    return (widened * inverse_rms * norm_gain[None, :]).astype(jnp.bfloat16)


def attention_kernel(
    core_ref, own_ref, other_ref, normed_ref, cosine_ref, sine_ref, positions_ref, cotangent_ref, grads_ref, rows_ref, weight_ref
):
    projected = project(core_ref, own_ref, other_ref, normed_ref, weight_ref, rows_ref)
    cosine, sine = cosine_ref[...], sine_ref[...]
    lower = lax.broadcasted_iota(jnp.int32, (128, 128), 1) < 64
    turned_sine = jnp.where(lower, -sine, sine)

    def rotate(part):
        return (part * cosine + pltpu.roll(part, 64, 1) * turned_sine).astype(jnp.bfloat16)

    def unrotate(part):
        return part * cosine + pltpu.roll(part * turned_sine, 64, 1)

    def product(left, right, over):
        return lax.dot_general(left, right, (((over[0],), (over[1],)), ((), ())), preferred_element_type=jnp.float32)

    queries, keys_rot = rotate(projected[:, :128]), rotate(projected[:, 128:256])
    values = projected[:, 256:].astype(jnp.bfloat16)
    cotangent = cotangent_ref[...]
    score_scale = 128 ** (-0.5)
    scores = product(queries, keys_rot, (1, 1)) * score_scale
    row_index = lax.broadcasted_iota(jnp.int32, (128, 128), 0)
    column_index = lax.broadcasted_iota(jnp.int32, (128, 128), 1)
    visible = (column_index <= row_index) & (row_index - column_index <= positions_ref[...])
    scores = jnp.where(visible, scores, -jnp.inf)
    exp_terms = jnp.exp(scores - jnp.max(scores, axis=1, keepdims=True))
    attention = exp_terms / jnp.sum(exp_terms, axis=1, keepdims=True)
    attention_low = attention.astype(jnp.bfloat16)
    prob_grad = product(cotangent, values, (1, 1))
    score_grad = (
        attention * (prob_grad - jnp.sum(attention * prob_grad, axis=1, keepdims=True)) * score_scale
    ).astype(jnp.bfloat16)
    grads = jnp.concatenate(
        [
            unrotate(product(score_grad, keys_rot, (1, 0))),
            unrotate(product(score_grad, queries, (0, 0))),
            product(attention_low, cotangent, (0, 0)),
        ],
        axis=1,
    ).astype(jnp.bfloat16)
    for copy in range(4):
        grads_ref[copy] = grads


def attention_grads(place, own, normed, tables, positions, cotangent):
    tokens, width = normed.shape[0], own.shape[1]
    raw = own.reshape(8, 2, 16, 8, width)
    ordered = pl.pallas_call(
        order_kernel,
        out_shape=jax.ShapeDtypeStruct((16, 2, 64, width), own.dtype),
        name="order_rows",
        compiler_params=SMALL,
        cost_estimate=BRIEF,
    )(raw)
    vmem = pl.BlockSpec(memory_space=pltpu.VMEM)
    grads, rows = pl.pallas_call(
        attention_kernel,
        out_shape=(
            jax.ShapeDtypeStruct((4, tokens, width), jnp.bfloat16),
            jax.ShapeDtypeStruct((512, width), jnp.bfloat16),
        ),
        in_specs=[pl.BlockSpec(memory_space=pltpu.SMEM)] + [vmem] * 7,
        out_specs=(vmem, vmem),
        scratch_shapes=[pltpu.VMEM((4096, width), jnp.bfloat16)],
        name="attention_grads",
        compiler_params=pltpu.CompilerParams(vmem_limit_bytes=20 * 2**20),
    )(place, ordered, swap_cores(ordered), normed, *tables, positions, cotangent)
    return grads.reshape(4 * tokens, width), rows


AXES = ("y_hi", "x", "z", "y_lo", "core")
FIRST_Z, LAST_Z = 12, 4
FIRST_ORDER, LAST_ORDER = ([[(place + start) % 16 for place in range(16)]] for start in (FIRST_Z, LAST_Z))
STEPS = 64.0
BRIEF = pl.CostEstimate(flops=2**20, bytes_accessed=2**18, transcendentals=0)
SMALL = pltpu.CompilerParams(vmem_limit_bytes=8 * 2**20)
FULL = 32767.0


def broadcast_rows(block, count):
    rows, width = block.shape
    return jnp.broadcast_to(block[None], (count, rows, width)).reshape(count * rows, width)


def swap_cores(array):
    return lax.ppermute(array, "core", [(0, 1), (1, 0)])


def copy_kernel(part_ref, copies_ref, seed_ref):
    late = FIRST_Z * 8
    for copy in range(16):
        copies_ref[copy, pl.ds(0, late), :] = part_ref[pl.ds(128 - late, late), :]
        copies_ref[copy, pl.ds(late, 128 - late), :] = part_ref[pl.ds(0, 128 - late), :]
    seed_ref[...] = jnp.zeros_like(seed_ref)


def gather_plane(qkv_weight):
    width = qkv_weight.shape[1]
    member = lax.axis_index("y_hi") * 4 + lax.axis_index("x")
    part = lax.dynamic_slice(qkv_weight, (member * 8, 0), (8, width))
    along_z = lax.all_to_all(broadcast_rows(part, 16), "z", 0, 0, axis_index_groups=FIRST_ORDER, tiled=True)
    copies, seed = pl.pallas_call(
        copy_kernel,
        out_shape=(jax.ShapeDtypeStruct((16, 128, width), jnp.bfloat16), jax.ShapeDtypeStruct((1, 512), jnp.bfloat16)),
        name="copy_rows",
        compiler_params=SMALL,
    )(along_z)
    plane = lax.all_to_all(copies.reshape(2048, width), ("y_hi", "x", "y_lo"), 0, 0, tiled=True)
    return seed, plane


def order_kernel(raw_ref, ordered_ref):
    for z in range(16):
        for y in range(2):
            rows = [raw_ref[eighth, y, z].astype(jnp.float32) for eighth in range(8)]
            ordered_ref[z, y] = jnp.concatenate(rows).astype(jnp.bfloat16)


def project(core_ref, own_ref, other_ref, normed_ref, weight_ref, rows_ref):
    core, column = core_ref[0], core_ref[1]
    for z in range(16):
        for y in range(2):
            place = z * 256 + y * 128
            weight_ref[pl.ds(pl.multiple_of(place + core * 64, 64), 64), :] = own_ref[z, y]
            weight_ref[pl.ds(pl.multiple_of(place + (1 - core) * 64, 64), 64), :] = other_ref[z, y]
    for half in range(2):
        start = pl.multiple_of(half * 2048 + column * 256, 256)
        rows_ref[pl.ds(half * 256, 256), :] = weight_ref[pl.ds(start, 256), :]
    return jnp.dot(normed_ref[...], weight_ref[...], preferred_element_type=jnp.float32)


def blocks_kernel(x_ref, activations_ref, *block_refs):
    squares = 0.0
    for part in range(4):
        widened = activations_ref[:, part * 1024 : (part + 1) * 1024].astype(jnp.float32)
        squares += jnp.sum(widened * widened, axis=1, keepdims=True)
    inverse_rms = jnp.broadcast_to(lax.rsqrt(squares / 4096 + norm_eps), (128, 128)).T
    high = inverse_rms.astype(jnp.bfloat16).astype(jnp.float32)
    rest = inverse_rms - high
    middle = rest.astype(jnp.bfloat16).astype(jnp.float32)
    row = lax.broadcasted_iota(jnp.int32, (128, 128), 0)
    extra = jnp.where(row == 0, high, jnp.where(row == 1, middle, jnp.where(row == 2, rest - middle, 0.0)))
    extra = jnp.concatenate([extra[:16]] * 4, axis=1).astype(jnp.bfloat16)
    for shift, block_ref in enumerate(block_refs):
        target = lax.rem(x_ref[0] + shift, 4)
        for half in range(2):
            start = pl.multiple_of(half * 2048 + target * 512, 512)
            block_ref[half, pl.ds(0, 128), :] = activations_ref[:, pl.ds(start, 512)]
            block_ref[half, pl.ds(128, 16), :] = extra


def redistribute(activations, x_index, core, seed):
    tokens = activations.shape[0]
    vmem = pl.BlockSpec(memory_space=pltpu.VMEM)
    blocks = pl.pallas_call(
        blocks_kernel,
        out_shape=[jax.ShapeDtypeStruct((2, tokens + 16, 512), jnp.bfloat16)] * 4,
        in_specs=[pl.BlockSpec(memory_space=pltpu.SMEM), vmem],
        out_specs=[vmem] * 4,
        name="cut_blocks",
        compiler_params=SMALL,
        cost_estimate=BRIEF,
    )(x_index.reshape(1), activations)
    ordered = jnp.broadcast_to(seed.reshape(1, 1, 1, 512), (4, 2, tokens + 16, 512))
    for shift in (0, 2, 1, 3):
        block = blocks[shift]
        if shift:
            block = lax.ppermute(block, "x", [(i, (i + shift) % 4) for i in range(4)])
        ordered = lax.dynamic_update_slice(ordered, block[None], (lax.rem(x_index - shift + 4, 4), 0, 0, 0))
    first, second = ordered[..., :256], ordered[..., 256:]
    kept = jnp.where(core == 0, first, second)
    sent = jnp.where(core == 0, second, first)
    return kept, swap_cores(sent)


def prepare_kernel(block_ref, gain_ref, normed_ref, unit_ref):
    for x in range(4):
        for half in range(2):
            block = block_ref[x, half].astype(jnp.float32)
            inverse_rms = (block[128:129, :128] + block[129:130, :128]) + block[130:131, :128]
            unit = block[:128].T * inverse_rms
            place = (pl.ds(half * 256, 256), pl.ds(x * 128, 128))
            unit_ref[place] = unit
            normed_ref[place] = (unit * gain_ref[pl.ds(half * 256, 256), :]).astype(jnp.bfloat16)


def prepared(block, gain_part):
    return pl.pallas_call(
        prepare_kernel,
        out_shape=(jax.ShapeDtypeStruct((512, 512), jnp.bfloat16), jax.ShapeDtypeStruct((512, 512), jnp.float32)),
        name="prepare_columns",
        compiler_params=pltpu.CompilerParams(vmem_limit_bytes=16 * 2**20),
    )(block, gain_part.reshape(512, 1))


def step_of(values, axis):
    peak = jnp.max(jnp.abs(values), axis=axis, keepdims=True)
    return jnp.clip(jnp.ceil(jnp.log2(peak) * STEPS), -110 * STEPS, 127 * STEPS)


def coded_values(values, step):
    return jnp.clip(jnp.round(values * (jnp.exp2(step * (-1 / STEPS)) * FULL)), -FULL, FULL)


def decoded_scale(step):
    return jnp.exp2(step * (1 / STEPS)) * (1 / FULL)


def coded_gain(gains):
    step = step_of(gains, -1)
    exact = gains * (jnp.exp2(step * (-1 / STEPS)) * FULL)
    high = jnp.clip(jnp.round(exact), -FULL, FULL)
    low = jnp.clip(jnp.round((exact - high) * FULL), -FULL, FULL)
    return high, low, jnp.broadcast_to(step, gains.shape)


def narrow(values):
    return values.astype(jnp.int32).astype(jnp.int16)


def wide(codes):
    return codes.astype(jnp.int32).astype(jnp.float32)


def half_grads(normed_ref, unit_ref, grads_ref, rows_ref):
    term = jnp.dot(normed_ref[...], grads_ref[...], preferred_element_type=jnp.float32)
    normed_grad = lax.dot_general(
        rows_ref[...], grads_ref[...], (((1,), (1,)), ((), ())), preferred_element_type=jnp.float32
    )
    return term, jnp.sum(normed_grad * unit_ref[...], axis=1, keepdims=True)


def first_grads_kernel(normed_ref, unit_ref, grads_ref, rows_ref, term_ref, gain_ref):
    term_ref[...], gain_ref[...] = half_grads(normed_ref, unit_ref, grads_ref, rows_ref)


def grads_kernel(first_ref, first_gain_ref, normed_ref, unit_ref, grads_ref, rows_ref, coded_ref, term_ref):
    term, gain = half_grads(normed_ref, unit_ref, grads_ref, rows_ref)
    term_ref[...] = first_ref[...] + term
    gain = first_gain_ref[...] + gain
    lanes = lax.broadcasted_iota(jnp.int32, (64, 128), 1)
    table = jnp.zeros((64, 128), jnp.float32)
    for chunk in range(8):
        first = chunk // 4 * 256 + chunk % 4 * 8
        column = jnp.concatenate([gain[first + z * 32 : first + z * 32 + 8] for z in range(8)])
        table = jnp.where(lanes == chunk, column, table)
    table = jnp.concatenate([table, jnp.zeros((64, 128), jnp.float32)]).T
    gains = coded_gain(table[:8])
    for chunk in range(8):
        first = chunk // 4 * 256 + chunk % 4 * 8
        rows = jnp.concatenate([term_ref[pl.ds(first + z * 32, 8), :] for z in range(8)])
        step = step_of(rows, 0)
        shown = [jnp.pad(part[chunk : chunk + 1], ((0, 0), (0, 256))) for part in gains]
        whole = [coded_values(rows, step), step] + shown + [jnp.zeros((4, 384), jnp.float32)]
        coded_ref[chunk] = narrow(jnp.concatenate(whole))


def code_z_kernel(parts_ref, coded_ref):
    rows, gains = [], []
    for core in range(2):
        row_sum, gain_sum = 0.0, 0.0
        for y in range(4):
            part = wide(parts_ref[y * 2 + core])
            extra = part[64:]
            row_sum += part[:64] * decoded_scale(extra[0:1])
            gain_sum += (extra[1:2, :128] + extra[2:3, :128] * (1 / FULL)) * decoded_scale(extra[3:4, :128])
        rows.append(row_sum)
        gains.append(gain_sum)
    rows = jnp.concatenate(rows).reshape(16, 8, 384)
    step = step_of(rows, 1)
    shown = jnp.concatenate(coded_gain(jnp.concatenate(gains)) + (jnp.zeros((2, 128), jnp.float32),))
    extra = []
    for z in range(16):
        moved = shown if z % 8 == 0 else pltpu.roll(shown, 128 - z % 8 * 8, 1)
        core = z // 8
        extra.append(jnp.concatenate(
            [step[z, :, k * 128 : (k + 1) * 128] for k in range(3)]
            + [moved[k + core : k + core + 1] for k in (0, 2, 4)]
            + [jnp.zeros((2, 128), jnp.float32)]
        ))
    whole = jnp.concatenate([coded_values(rows, step).reshape(128, 384), jnp.concatenate(extra)], axis=1)
    coded_ref[...] = narrow(jnp.concatenate([whole[LAST_Z * 8 :], whole[: LAST_Z * 8]]))


def decode_kernel(coded_ref, rows_ref, gains_ref):
    whole = wide(coded_ref[...]).reshape(16, 8, 512)
    extra = whole[:, :, 384:]
    step = jnp.concatenate([extra[:, 0:1], extra[:, 1:2], extra[:, 2:3]], axis=2)
    rows_ref[...] = jnp.sum(whole[:, :, :384] * decoded_scale(step), axis=0)
    gains = (extra[:, 3:4] + extra[:, 4:5] * (1 / FULL)) * decoded_scale(extra[:, 5:6])
    gains_ref[...] = jnp.sum(gains, axis=0)[:, :8]


def shards(activations, norm_gain, qkv_weight, positions, cotangent):
    x_index = lax.axis_index("x")
    core = lax.axis_index("core")
    width = qkv_weight.shape[1]
    tokens = activations.shape[0]
    seed, own_weight = gather_plane(qkv_weight)
    normed = normalize(activations + jnp.tile(seed, (1, 8)), norm_gain)
    kept, received = redistribute(activations, x_index, core, seed)
    gain_part = lax.dynamic_slice(norm_gain.reshape(2, 8, 256), (0, x_index * 2 + core, 0), (2, 1, 256)).reshape(512)
    kept = prepared(kept, gain_part)
    received = prepared(received, gain_part)
    own_weight, normed, kept, received = lax.optimization_barrier((own_weight, normed, kept, received))
    positions = positions.reshape(tokens, 1)
    tables = rope_tables(positions, cotangent.shape[1], own_weight)

    place = jnp.stack([core, x_index * 2 + core])
    qkv_grads, weight_rows = attention_grads(place, own_weight, normed, tables, positions, cotangent)

    own_grads = lax.all_to_all(qkv_grads, "x", 0, 0, tiled=True)
    other_grads = swap_cores(own_grads)

    first = pl.pallas_call(
        first_grads_kernel,
        out_shape=(jax.ShapeDtypeStruct((512, width), jnp.float32), jax.ShapeDtypeStruct((512, 1), jnp.float32)),
        name="first_grads",
        compiler_params=pltpu.CompilerParams(vmem_limit_bytes=16 * 2**20),
        cost_estimate=BRIEF,
    )(*kept, own_grads, weight_rows)
    parts = pl.pallas_call(
        grads_kernel,
        out_shape=jax.ShapeDtypeStruct((8, 72, width), jnp.int16),
        scratch_shapes=[pltpu.VMEM((512, width), jnp.float32)],
        name="code_y",
        compiler_params=pltpu.CompilerParams(vmem_limit_bytes=16 * 2**20),
    )(*first, *received, other_grads, weight_rows)
    parts = lax.all_to_all(parts, ("y_hi", "y_lo", "core"), 0, 0, tiled=True)
    coded = pl.pallas_call(
        code_z_kernel, out_shape=jax.ShapeDtypeStruct((128, 512), jnp.int16), name="code_z", compiler_params=SMALL
    )(parts)
    coded = lax.all_to_all(coded, "z", 0, 0, axis_index_groups=LAST_ORDER, tiled=True)
    share, gains = pl.pallas_call(
        decode_kernel,
        out_shape=(jax.ShapeDtypeStruct((8, width), jnp.float32), jax.ShapeDtypeStruct((1, 8), jnp.float32)),
        name="decode_rows", compiler_params=SMALL,
    )(coded)
    return share, gains.reshape(8)


def solution(mesh):
    fine = Mesh(mesh.devices.reshape(2, 4, 16, 2, 2), AXES)
    placed = (
        P(AXES, None),
        P(),
        P(("z", "y_lo", "core"), None),
        P(AXES),
        P(AXES, None),
    )
    return jax.shard_map(
        shards,
        mesh=fine,
        in_specs=placed,
        out_specs=(P(AXES, None), P(AXES)),
        check_vma=False,
    )
```

```python
import jax
import jax.numpy as jnp
from jax import lax
from jax.experimental import pallas as pl
from jax.experimental.pallas import tpu as pltpu
from jax.sharding import Mesh, PartitionSpec as P

rope_base = 10000.0
norm_eps = 1e-05


def angle_kernel(positions_ref, frequency_ref, after_ref, angles_ref):
    angles_ref[...] = positions_ref[...].astype(jnp.float32) * frequency_ref[...]


def rope_tables(positions, head_size, after):
    half_width = head_size // 2
    exponent = jnp.arange(half_width, dtype=jnp.float32) * (-2.0 / head_size)
    frequency = jnp.power(jnp.float32(rope_base), exponent)
    frequency = jnp.concatenate([frequency, frequency])[None]
    vmem = pl.BlockSpec(memory_space=pltpu.VMEM)
    angle_table = pl.pallas_call(
        angle_kernel,
        out_shape=jax.ShapeDtypeStruct((positions.shape[0], head_size), jnp.float32),
        in_specs=[vmem, vmem, pl.BlockSpec(memory_space=pl.ANY)],
        out_specs=vmem,
        name="angles",
        compiler_params=SMALL,
        cost_estimate=BRIEF,
    )(positions, frequency, after)
    return (jnp.cos(angle_table), jnp.sin(angle_table))


def normalize(activations, norm_gain):
    widened = activations.astype(jnp.float32)
    inverse_rms = lax.rsqrt(jnp.mean(widened * widened, axis=1, keepdims=True) + norm_eps)
    return (widened * inverse_rms * norm_gain[None, :]).astype(jnp.bfloat16)


def attention_kernel(
    core_ref, own_ref, other_ref, normed_ref, cosine_ref, sine_ref, positions_ref, cotangent_ref, grads_ref, rows_ref, weight_ref
):
    projected = project(core_ref, own_ref, other_ref, normed_ref, weight_ref, rows_ref)
    cosine, sine = cosine_ref[...], sine_ref[...]
    lower = lax.broadcasted_iota(jnp.int32, (128, 128), 1) < 64
    turned_sine = jnp.where(lower, -sine, sine)

    def rotate(part):
        return (part * cosine + pltpu.roll(part, 64, 1) * turned_sine).astype(jnp.bfloat16)

    def unrotate(part):
        return part * cosine + pltpu.roll(part * turned_sine, 64, 1)

    def product(left, right, over):
        return lax.dot_general(left, right, (((over[0],), (over[1],)), ((), ())), preferred_element_type=jnp.float32)

    queries, keys_rot = rotate(projected[:, :128]), rotate(projected[:, 128:256])
    values = projected[:, 256:].astype(jnp.bfloat16)
    cotangent = cotangent_ref[...]
    score_scale = 128 ** (-0.5)
    scores = product(queries, keys_rot, (1, 1)) * score_scale
    row_index = lax.broadcasted_iota(jnp.int32, (128, 128), 0)
    column_index = lax.broadcasted_iota(jnp.int32, (128, 128), 1)
    visible = (column_index <= row_index) & (row_index - column_index <= positions_ref[...])
    scores = jnp.where(visible, scores, -jnp.inf)
    exp_terms = jnp.exp(scores - jnp.max(scores, axis=1, keepdims=True))
    attention = exp_terms / jnp.sum(exp_terms, axis=1, keepdims=True)
    attention_low = attention.astype(jnp.bfloat16)
    prob_grad = product(cotangent, values, (1, 1))
    score_grad = (
        attention * (prob_grad - jnp.sum(attention * prob_grad, axis=1, keepdims=True)) * score_scale
    ).astype(jnp.bfloat16)
    grads = jnp.concatenate(
        [
            unrotate(product(score_grad, keys_rot, (1, 0))),
            unrotate(product(score_grad, queries, (0, 0))),
            product(attention_low, cotangent, (0, 0)),
        ],
        axis=1,
    ).astype(jnp.bfloat16)
    for copy in range(4):
        grads_ref[copy] = grads


def attention_grads(place, own, normed, tables, positions, cotangent):
    tokens, width = normed.shape[0], own.shape[1]
    raw = own.reshape(8, 2, 16, 8, width)
    ordered = pl.pallas_call(
        order_kernel,
        out_shape=jax.ShapeDtypeStruct((16, 2, 64, width), own.dtype),
        name="order_rows",
        compiler_params=SMALL,
        cost_estimate=BRIEF,
    )(raw)
    vmem = pl.BlockSpec(memory_space=pltpu.VMEM)
    grads, rows = pl.pallas_call(
        attention_kernel,
        out_shape=(
            jax.ShapeDtypeStruct((4, tokens, width), jnp.bfloat16),
            jax.ShapeDtypeStruct((512, width), jnp.bfloat16),
        ),
        in_specs=[pl.BlockSpec(memory_space=pltpu.SMEM)] + [vmem] * 7,
        out_specs=(vmem, vmem),
        scratch_shapes=[pltpu.VMEM((4096, width), jnp.bfloat16)],
        name="attention_grads",
        compiler_params=pltpu.CompilerParams(vmem_limit_bytes=20 * 2**20),
    )(place, ordered, swap_cores(ordered), normed, *tables, positions, cotangent)
    return grads.reshape(4 * tokens, width), rows


AXES = ("y_hi", "x", "z", "y_lo", "core")
FIRST_Z, LAST_Z = 12, 4
FIRST_ORDER, LAST_ORDER = ([[(place + start) % 16 for place in range(16)]] for start in (FIRST_Z, LAST_Z))
STEPS = 64.0
BRIEF = pl.CostEstimate(flops=2**20, bytes_accessed=2**18, transcendentals=0)
SMALL = pltpu.CompilerParams(vmem_limit_bytes=8 * 2**20)
FULL = 32767.0


def broadcast_rows(block, count):
    rows, width = block.shape
    return jnp.broadcast_to(block[None], (count, rows, width)).reshape(count * rows, width)


def swap_cores(array):
    return lax.ppermute(array, "core", [(0, 1), (1, 0)])


def part_kernel(member_ref, weight_ref, parts_ref, wide_ref):
    wide_ref[...] = weight_ref[...].astype(jnp.float32)
    rows = wide_ref[pl.ds(pl.multiple_of(member_ref[0] * 8, 8), 8), :].astype(jnp.bfloat16)
    for copy in range(16):
        parts_ref[copy] = rows


def copy_kernel(part_ref, copies_ref, seed_ref):
    late = FIRST_Z * 8
    for copy in range(16):
        copies_ref[copy, pl.ds(0, late), :] = part_ref[pl.ds(128 - late, late), :]
        copies_ref[copy, pl.ds(late, 128 - late), :] = part_ref[pl.ds(0, 128 - late), :]
    seed_ref[...] = jnp.zeros_like(seed_ref)


def gather_plane(qkv_weight):
    width = qkv_weight.shape[1]
    member = lax.axis_index("y_hi") * 4 + lax.axis_index("x")
    parts = pl.pallas_call(
        part_kernel,
        out_shape=jax.ShapeDtypeStruct((16, 8, width), jnp.bfloat16),
        in_specs=[pl.BlockSpec(memory_space=pltpu.SMEM), pl.BlockSpec(memory_space=pltpu.VMEM)],
        out_specs=pl.BlockSpec(memory_space=pltpu.VMEM),
        scratch_shapes=[pltpu.VMEM((64, width), jnp.float32)],
        name="part_rows",
        compiler_params=SMALL,
        cost_estimate=BRIEF,
    )(member.reshape(1), qkv_weight)
    along_z = lax.all_to_all(parts.reshape(128, width), "z", 0, 0, axis_index_groups=FIRST_ORDER, tiled=True)
    copies, seed = pl.pallas_call(
        copy_kernel,
        out_shape=(jax.ShapeDtypeStruct((16, 128, width), jnp.bfloat16), jax.ShapeDtypeStruct((1, 512), jnp.bfloat16)),
        name="copy_rows",
        compiler_params=SMALL,
    )(along_z)
    plane = lax.all_to_all(copies.reshape(2048, width), ("y_hi", "x", "y_lo"), 0, 0, tiled=True)
    return seed, plane


def order_kernel(raw_ref, ordered_ref):
    for z in range(16):
        for y in range(2):
            rows = [raw_ref[eighth, y, z].astype(jnp.float32) for eighth in range(8)]
            ordered_ref[z, y] = jnp.concatenate(rows).astype(jnp.bfloat16)


def project(core_ref, own_ref, other_ref, normed_ref, weight_ref, rows_ref):
    core, column = core_ref[0], core_ref[1]
    for z in range(16):
        for y in range(2):
            place = z * 256 + y * 128
            weight_ref[pl.ds(pl.multiple_of(place + core * 64, 64), 64), :] = own_ref[z, y]
            weight_ref[pl.ds(pl.multiple_of(place + (1 - core) * 64, 64), 64), :] = other_ref[z, y]
    for half in range(2):
        start = pl.multiple_of(half * 2048 + column * 256, 256)
        rows_ref[pl.ds(half * 256, 256), :] = weight_ref[pl.ds(start, 256), :]
    return jnp.dot(normed_ref[...], weight_ref[...], preferred_element_type=jnp.float32)


def blocks_kernel(x_ref, activations_ref, *block_refs):
    squares = 0.0
    for part in range(4):
        widened = activations_ref[:, part * 1024 : (part + 1) * 1024].astype(jnp.float32)
        squares += jnp.sum(widened * widened, axis=1, keepdims=True)
    inverse_rms = jnp.broadcast_to(lax.rsqrt(squares / 4096 + norm_eps), (128, 128)).T
    high = inverse_rms.astype(jnp.bfloat16).astype(jnp.float32)
    rest = inverse_rms - high
    middle = rest.astype(jnp.bfloat16).astype(jnp.float32)
    row = lax.broadcasted_iota(jnp.int32, (128, 128), 0)
    extra = jnp.where(row == 0, high, jnp.where(row == 1, middle, jnp.where(row == 2, rest - middle, 0.0)))
    extra = jnp.concatenate([extra[:16]] * 4, axis=1).astype(jnp.bfloat16)
    for shift, block_ref in enumerate(block_refs):
        target = lax.rem(x_ref[0] + shift, 4)
        for half in range(2):
            start = pl.multiple_of(half * 2048 + target * 512, 512)
            block_ref[half, pl.ds(0, 128), :] = activations_ref[:, pl.ds(start, 512)]
            block_ref[half, pl.ds(128, 16), :] = extra


def redistribute(activations, x_index, core, seed):
    tokens = activations.shape[0]
    vmem = pl.BlockSpec(memory_space=pltpu.VMEM)
    blocks = pl.pallas_call(
        blocks_kernel,
        out_shape=[jax.ShapeDtypeStruct((2, tokens + 16, 512), jnp.bfloat16)] * 4,
        in_specs=[pl.BlockSpec(memory_space=pltpu.SMEM), vmem],
        out_specs=[vmem] * 4,
        name="cut_blocks",
        compiler_params=SMALL,
        cost_estimate=BRIEF,
    )(x_index.reshape(1), activations)
    ordered = jnp.broadcast_to(seed.reshape(1, 1, 1, 512), (4, 2, tokens + 16, 512))
    for shift in (0, 2, 1, 3):
        block = blocks[shift]
        if shift:
            block = lax.ppermute(block, "x", [(i, (i + shift) % 4) for i in range(4)])
        ordered = lax.dynamic_update_slice(ordered, block[None], (lax.rem(x_index - shift + 4, 4), 0, 0, 0))
    first, second = ordered[..., :256], ordered[..., 256:]
    kept = jnp.where(core == 0, first, second)
    sent = jnp.where(core == 0, second, first)
    return kept, swap_cores(sent)


def prepare_kernel(block_ref, gain_ref, normed_ref, unit_ref):
    for x in range(4):
        for half in range(2):
            block = block_ref[x, half].astype(jnp.float32)
            inverse_rms = (block[128:129, :128] + block[129:130, :128]) + block[130:131, :128]
            unit = block[:128].T * inverse_rms
            place = (pl.ds(half * 256, 256), pl.ds(x * 128, 128))
            unit_ref[place] = unit
            normed_ref[place] = (unit * gain_ref[pl.ds(half * 256, 256), :]).astype(jnp.bfloat16)


def prepared(block, gain_part):
    return pl.pallas_call(
        prepare_kernel,
        out_shape=(jax.ShapeDtypeStruct((512, 512), jnp.bfloat16), jax.ShapeDtypeStruct((512, 512), jnp.float32)),
        name="prepare_columns",
        compiler_params=pltpu.CompilerParams(vmem_limit_bytes=16 * 2**20),
    )(block, gain_part.reshape(512, 1))


def step_of(values, axis):
    peak = jnp.max(jnp.abs(values), axis=axis, keepdims=True)
    return jnp.clip(jnp.ceil(jnp.log2(peak) * STEPS), -110 * STEPS, 127 * STEPS)


def coded_values(values, step):
    return jnp.clip(jnp.round(values * (jnp.exp2(step * (-1 / STEPS)) * FULL)), -FULL, FULL)


def decoded_scale(step):
    return jnp.exp2(step * (1 / STEPS)) * (1 / FULL)


def coded_gain(gains):
    step = step_of(gains, -1)
    exact = gains * (jnp.exp2(step * (-1 / STEPS)) * FULL)
    high = jnp.clip(jnp.round(exact), -FULL, FULL)
    low = jnp.clip(jnp.round((exact - high) * FULL), -FULL, FULL)
    return high, low, jnp.broadcast_to(step, gains.shape)


def narrow(values):
    return values.astype(jnp.int32).astype(jnp.int16)


def wide(codes):
    return codes.astype(jnp.int32).astype(jnp.float32)


def half_grads(normed_ref, unit_ref, grads_ref, rows_ref):
    term = jnp.dot(normed_ref[...], grads_ref[...], preferred_element_type=jnp.float32)
    normed_grad = lax.dot_general(
        rows_ref[...], grads_ref[...], (((1,), (1,)), ((), ())), preferred_element_type=jnp.float32
    )
    return term, jnp.sum(normed_grad * unit_ref[...], axis=1, keepdims=True)


def first_grads_kernel(normed_ref, unit_ref, grads_ref, rows_ref, term_ref, gain_ref):
    term_ref[...], gain_ref[...] = half_grads(normed_ref, unit_ref, grads_ref, rows_ref)


def grads_kernel(first_ref, first_gain_ref, normed_ref, unit_ref, grads_ref, rows_ref, coded_ref, term_ref):
    term, gain = half_grads(normed_ref, unit_ref, grads_ref, rows_ref)
    term_ref[...] = first_ref[...] + term
    gain = first_gain_ref[...] + gain
    lanes = lax.broadcasted_iota(jnp.int32, (64, 128), 1)
    table = jnp.zeros((64, 128), jnp.float32)
    for chunk in range(8):
        first = chunk // 4 * 256 + chunk % 4 * 8
        column = jnp.concatenate([gain[first + z * 32 : first + z * 32 + 8] for z in range(8)])
        table = jnp.where(lanes == chunk, column, table)
    table = jnp.concatenate([table, jnp.zeros((64, 128), jnp.float32)]).T
    gains = coded_gain(table[:8])
    for chunk in range(8):
        first = chunk // 4 * 256 + chunk % 4 * 8
        rows = jnp.concatenate([term_ref[pl.ds(first + z * 32, 8), :] for z in range(8)])
        step = step_of(rows, 0)
        shown = [jnp.pad(part[chunk : chunk + 1], ((0, 0), (0, 256))) for part in gains]
        whole = [coded_values(rows, step), step] + shown + [jnp.zeros((4, 384), jnp.float32)]
        coded_ref[chunk] = narrow(jnp.concatenate(whole))


def code_z_kernel(parts_ref, coded_ref):
    rows, gains = [], []
    for core in range(2):
        row_sum, gain_sum = 0.0, 0.0
        for y in range(4):
            part = wide(parts_ref[y * 2 + core])
            extra = part[64:]
            row_sum += part[:64] * decoded_scale(extra[0:1])
            gain_sum += (extra[1:2, :128] + extra[2:3, :128] * (1 / FULL)) * decoded_scale(extra[3:4, :128])
        rows.append(row_sum)
        gains.append(gain_sum)
    rows = jnp.concatenate(rows).reshape(16, 8, 384)
    step = step_of(rows, 1)
    shown = jnp.concatenate(coded_gain(jnp.concatenate(gains)) + (jnp.zeros((2, 128), jnp.float32),))
    extra = []
    for z in range(16):
        moved = shown if z % 8 == 0 else pltpu.roll(shown, 128 - z % 8 * 8, 1)
        core = z // 8
        extra.append(jnp.concatenate(
            [step[z, :, k * 128 : (k + 1) * 128] for k in range(3)]
            + [moved[k + core : k + core + 1] for k in (0, 2, 4)]
            + [jnp.zeros((2, 128), jnp.float32)]
        ))
    whole = jnp.concatenate([coded_values(rows, step).reshape(128, 384), jnp.concatenate(extra)], axis=1)
    coded_ref[...] = narrow(jnp.concatenate([whole[LAST_Z * 8 :], whole[: LAST_Z * 8]]))


def decode_kernel(coded_ref, rows_ref, gains_ref):
    whole = wide(coded_ref[...]).reshape(16, 8, 512)
    extra = whole[:, :, 384:]
    step = jnp.concatenate([extra[:, 0:1], extra[:, 1:2], extra[:, 2:3]], axis=2)
    rows_ref[...] = jnp.sum(whole[:, :, :384] * decoded_scale(step), axis=0)
    gains = (extra[:, 3:4] + extra[:, 4:5] * (1 / FULL)) * decoded_scale(extra[:, 5:6])
    gains_ref[...] = jnp.sum(gains, axis=0)[:, :8]


def shards(activations, norm_gain, qkv_weight, positions, cotangent):
    x_index = lax.axis_index("x")
    core = lax.axis_index("core")
    width = qkv_weight.shape[1]
    tokens = activations.shape[0]
    seed, own_weight = gather_plane(qkv_weight)
    normed = normalize(activations + jnp.tile(seed, (1, 8)), norm_gain)
    kept, received = redistribute(activations, x_index, core, seed)
    gain_part = lax.dynamic_slice(norm_gain.reshape(2, 8, 256), (0, x_index * 2 + core, 0), (2, 1, 256)).reshape(512)
    kept = prepared(kept, gain_part)
    received = prepared(received, gain_part)
    own_weight, normed, kept, received = lax.optimization_barrier((own_weight, normed, kept, received))
    positions = positions.reshape(tokens, 1)
    tables = rope_tables(positions, cotangent.shape[1], own_weight)

    place = jnp.stack([core, x_index * 2 + core])
    qkv_grads, weight_rows = attention_grads(place, own_weight, normed, tables, positions, cotangent)

    own_grads = lax.all_to_all(qkv_grads, "x", 0, 0, tiled=True)
    other_grads = swap_cores(own_grads)

    first = pl.pallas_call(
        first_grads_kernel,
        out_shape=(jax.ShapeDtypeStruct((512, width), jnp.float32), jax.ShapeDtypeStruct((512, 1), jnp.float32)),
        name="first_grads",
        compiler_params=pltpu.CompilerParams(vmem_limit_bytes=16 * 2**20),
        cost_estimate=BRIEF,
    )(*kept, own_grads, weight_rows)
    parts = pl.pallas_call(
        grads_kernel,
        out_shape=jax.ShapeDtypeStruct((8, 72, width), jnp.int16),
        scratch_shapes=[pltpu.VMEM((512, width), jnp.float32)],
        name="code_y",
        compiler_params=pltpu.CompilerParams(vmem_limit_bytes=16 * 2**20),
    )(*first, *received, other_grads, weight_rows)
    parts = lax.all_to_all(parts, ("y_hi", "y_lo", "core"), 0, 0, tiled=True)
    coded = pl.pallas_call(
        code_z_kernel, out_shape=jax.ShapeDtypeStruct((128, 512), jnp.int16), name="code_z", compiler_params=SMALL
    )(parts)
    coded = lax.all_to_all(coded, "z", 0, 0, axis_index_groups=LAST_ORDER, tiled=True)
    share, gains = pl.pallas_call(
        decode_kernel,
        out_shape=(jax.ShapeDtypeStruct((8, width), jnp.float32), jax.ShapeDtypeStruct((1, 8), jnp.float32)),
        name="decode_rows", compiler_params=SMALL,
    )(coded)
    return share, gains.reshape(8)


def solution(mesh):
    fine = Mesh(mesh.devices.reshape(2, 4, 16, 2, 2), AXES)
    placed = (
        P(AXES, None),
        P(),
        P(("z", "y_lo", "core"), None),
        P(AXES),
        P(AXES, None),
    )
    return jax.shard_map(
        shards,
        mesh=fine,
        in_specs=placed,
        out_specs=(P(AXES, None), P(AXES)),
        check_vma=False,
    )
```
